32 devices in a mesh: section: 2 (over x), replica: 16 (over z, y, core).
Axes of the slice: x: 2, y: 2, z: 4, core: 2. Of those that a mesh axis runs over, the one named last changes fastest.
Arguments:
- pending_section_entries: bfloat16 [2, 32, 14, 14, 512], P('section', 'replica'), may hold values from -40 to 40
- arriving_microsets: bfloat16 [1, 32, 14, 14, 512], P(None, 'replica'), may hold values from -40 to 40
- opening_filter_kernel: bfloat16 [2, 3, 3, 512, 512], P('section'), may hold values from -0.09375 to 0.09375
- closing_filter_kernel: bfloat16 [2, 3, 3, 512, 512], P('section'), may hold values from -0.09375 to 0.09375
- stretch_factors: float32 [2, 2, 512], P('section'), may hold values from 0.5 to 1.5
- shift_terms: float32 [2, 2, 512], P('section'), may hold values from -3 to 3
Outputs:
- produced: bfloat16 [2, 2, 32, 14, 14, 512], P('section', None, 'replica')
The draws below stay inside these ranges and needn't reach their ends.
All inputs are finite; a program needn't handle non-finite values.
Results may differ from the reference program's by a relative error of at most 0.0084.
Values may be sent and summed in bfloat16 or wider, within the bound.
A program may use at most 64 MiB of HBM per device.

```python
import jax
import jax.numpy as jnp
from jax import lax

C = 512
H = 14
W = 14
IMG_DEV = 2
TICKS = 2
SECTIONS = 2
IMAGES = 32


def replica_pattern(count):
    owner = jnp.arange(count) // IMG_DEV
    parity = jnp.where(owner % 2 == 1, 1.8, 1.0 / 1.8)
    triple = jnp.where(owner % 3 == 0, 1.6, 0.8)
    return (parity * triple).astype(jnp.float32)


def image_scales(key, count):
    steps = jnp.arange(count).astype(jnp.float32) / max(count - 1, 1)
    spread = 3.0 ** steps
    return spread * replica_pattern(count)


def draw_field(key, lead):
    keys = jax.random.split(key, 3)
    tensor_shape = (lead, IMAGES, H, W, C)
    base = jax.random.normal(keys[0], tensor_shape, jnp.float32)
    pixel = jnp.exp(jax.random.uniform(keys[1], (lead, IMAGES, H, W, 1), jnp.float32) * jnp.log(10.0)) / 3.0
    norm_scales = image_scales(keys[2], IMAGES).reshape(1, IMAGES, 1, 1, 1)
    return jnp.clip(base * pixel * norm_scales, -40.0, 40.0)


def draw_pending_section_entries(key, part):
    return draw_field(jax.random.fold_in(key, 11), SECTIONS).astype(jnp.bfloat16)


def draw_arriving_microsets(key, part):
    return draw_field(jax.random.fold_in(key, 23), TICKS - 1).astype(jnp.bfloat16)


def shard_levels(own_key, extent, cuts, low, largest):
    level, own = 1.0, jax.random.fold_in(own_key, 6)
    for dim, shards_of in cuts:
        draws = jnp.exp(jax.random.uniform(jax.random.fold_in(own, dim), (shards_of,), jnp.float32, low / len(cuts), largest / len(cuts)))
        level = level * jnp.repeat(draws, extent[dim] // shards_of).reshape([-1 if axis == dim else 1 for axis in range(len(extent))])
    return level


def gaussian(key, shape, deviation, bound, pieces=(), kind=jnp.bfloat16):
    entries = deviation * jax.random.normal(key, shape, jnp.float32)
    if pieces:
        entries = entries * shard_levels(key, shape, pieces, -0.22, 0.18)
    return jnp.clip(entries, -bound, bound).astype(kind)


def setup_inputs(seed: int = 0) -> dict:
    key_list = jax.random.split(jax.random.key(seed), 7)
    pending_section_entries = draw_pending_section_entries(jax.random.fold_in(key_list[6], 71), 0)
    arriving_microsets = draw_arriving_microsets(jax.random.fold_in(key_list[6], 71), 0)
    opening_filter_kernel = gaussian(key_list[2], (SECTIONS, 3, 3, C, C), (9 * C) ** -0.5, 0.09375, ((0, 2),))
    closing_filter_kernel = gaussian(key_list[3], (SECTIONS, 3, 3, C, C), (9 * C) ** -0.5, 0.09375, ((0, 2),))
    stretch_factors = jnp.clip(0.5 + 1.0 * jax.random.uniform(key_list[4], (SECTIONS, 2, C), jnp.float32) ** shard_levels(key_list[4], (SECTIONS, 2, C), ((0, 2),), -0.2, 0.2), 0.5, 1.5)
    shift_terms = gaussian(key_list[5], (SECTIONS, 2, C), 0.5, 3.0, ((0, 2),), jnp.float32)
    return dict(pending_section_entries=pending_section_entries, arriving_microsets=arriving_microsets, opening_filter_kernel=opening_filter_kernel, closing_filter_kernel=closing_filter_kernel, stretch_factors=stretch_factors, shift_terms=shift_terms)


def convolve(maps, kernel):
    return lax.conv_general_dilated(maps, kernel, (1, 1), 'SAME', dimension_numbers=('NHWC', 'HWIO', 'NHWC'), preferred_element_type=jnp.float32)

def layer(maps, kernel, gain, bias):
    conv_out = convolve(maps, kernel)
    mean = lax.optimization_barrier(jnp.mean(conv_out, axis=(0, 1, 2)))
    centred = conv_out - mean
    var = lax.optimization_barrier(jnp.mean(centred * centred, axis=(0, 1, 2)))
    scale = gain * lax.rsqrt(var + 1e-05)
    offset = bias - mean * scale
    stored = lax.optimization_barrier(conv_out.astype(jnp.bfloat16)).astype(jnp.float32)
    return jnp.maximum(stored * scale + offset, 0.0).astype(jnp.bfloat16)

def section_step(packed):
    maps, first, second, gain, bias = packed
    hidden = layer(maps, first, gain[0], bias[0])
    return layer(hidden, second, gain[1], bias[1])

def reference(pending_section_entries, arriving_microsets, opening_filter_kernel, closing_filter_kernel, stretch_factors, shift_terms):
    feed_examples = pending_section_entries
    results = []
    for tick in range(TICKS):
        outputs = lax.map(section_step, (feed_examples, opening_filter_kernel, closing_filter_kernel, stretch_factors, shift_terms))
        results.append(outputs)
        if tick + 1 < TICKS:
            feed_examples = jnp.concatenate([arriving_microsets[tick][None], outputs[:-1]], axis=0)
    return jnp.stack(results, axis=1)
```

```python
import functools

import jax
import jax.numpy as jnp
from jax import lax
from jax.experimental import pallas as pl
from jax.experimental.pallas import tpu as pltpu
from jax.sharding import PartitionSpec as P

MESH = pl.DeviceIdType.MESH
F32 = jnp.float32
BF16 = jnp.bfloat16
LANES = 128
PITCH = 16
TILE = 256


def kernel(
    sections,
    replicas,
    pend,
    arriving,
    first,
    second,
    gain,
    bias,
    out,
    maps,
    weights,
    taps,
    y,
    sent,
    landed,
    mine,
    slots,
    coef,
    moved_coef,
    affine,
    result,
    map_sem,
    weight_sem,
    out_sem,
    stat_send,
    stat_recv,
    bulk_send,
    bulk_recv,
    coef_send,
    coef_recv,
):
    images, rows, cols, channels = maps.shape[1:]
    chunks = channels // LANES
    halves = channels // TILE
    blocks = y.shape[0]
    cells = images * rows * cols
    sec = lax.axis_index("section")
    me = lax.axis_index("replica")

    barrier = pltpu.get_barrier_semaphore()

    def greet(d, carry):
        peer = lax.rem(me + d, replicas)
        pl.semaphore_signal(
            barrier, inc=1, device_id={"section": sec, "replica": peer}, device_id_type=MESH
        )
        return carry

    lax.fori_loop(1, replicas, greet, 0)

    @pl.when(sec > 0)
    def _():
        pl.semaphore_signal(
            barrier, inc=1, device_id={"section": sec - 1, "replica": me}, device_id_type=MESH
        )

    @pl.when(sec < sections - 1)
    def _():
        pl.semaphore_signal(
            barrier, inc=1, device_id={"section": sec + 1, "replica": me}, device_id_type=MESH
        )

    map_copies = [
        pltpu.make_async_copy(pend.at[0], maps.at[0], map_sem.at[0]),
        pltpu.make_async_copy(arriving.at[0], maps.at[1], map_sem.at[1]),
    ]
    weight_copies = [
        [
            pltpu.make_async_copy(src.at[0, dy], weights.at[layer, dy], weight_sem.at[layer, dy])
            for dy in range(3)
        ]
        for layer, src in enumerate((first, second))
    ]
    map_copies[0].start()
    for layer in range(2):
        for dy in range(3):
            weight_copies[layer][dy].start()
    map_copies[1].start()

    for layer in range(2):
        for k in range(chunks):
            lane = slice(k * LANES, (k + 1) * LANES)
            affine[layer, k : k + 1, :] = gain[0, layer : layer + 1, lane]
            affine[layer, chunks + k : chunks + k + 1, :] = bias[0, layer : layer + 1, lane]

    pad = jnp.zeros((halves, PITCH, 3 * TILE), BF16)
    for i in range(images + 1):
        at = i * (rows + 1) * PITCH
        taps[:, at : at + PITCH, :] = pad

    inside = lax.broadcasted_iota(jnp.int32, (rows, PITCH, LANES), 1) < cols

    def lay(i, k, values):
        flat = jnp.where(inside, values, 0.0).reshape(rows * PITCH, LANES)
        at = (i * (rows + 1) + 1) * PITCH
        half, lane = (k * LANES) // TILE, (k * LANES) % TILE
        where = slice(at, at + rows * PITCH)
        taps[half, where, lane : lane + LANES] = pltpu.roll(flat, 1, 0).astype(BF16)
        taps[half, where, TILE + lane : TILE + lane + LANES] = flat.astype(BF16)
        taps[half, where, 2 * TILE + lane : 2 * TILE + lane + LANES] = pltpu.roll(
            flat, rows * PITCH - 1, 0
        ).astype(BF16)

    def block_rows(i):
        return slice(i * (rows + 1), i * (rows + 1) + rows)

    def lay_maps(which):
        for i in range(images):
            for k in range(chunks):
                lane = slice(k * LANES, (k + 1) * LANES)
                y[block_rows(i), 0:cols, lane] = maps[which, i, :, :, lane].astype(F32)
                lay(i, k, y[block_rows(i), :, lane])

    def multiply(layer, n, parts, add):
        lane = slice(n * TILE, (n + 1) * TILE)
        total = None
        for dy, half in parts:
            left = taps[half, dy * PITCH : (dy + blocks) * PITCH, :]
            right = weights[layer, dy, :, half * TILE : (half + 1) * TILE, lane]
            term = jnp.dot(left, right.reshape(3 * TILE, TILE), preferred_element_type=F32)
            total = term if total is None else total + term
        total = total.reshape(blocks, PITCH, TILE)
        y[:, :, lane] = y[:, :, lane] + total if add else total

    every = [(dy, half) for half in range(halves) for dy in range(3)]

    def gather_statistics(phase):
        for k in range(chunks):
            lane = slice(k * LANES, (k + 1) * LANES)
            total = 0.0
            for i in range(images):
                total = total + jnp.sum(jnp.where(inside, y[block_rows(i), :, lane], 0.0), axis=0)
            mean = jnp.sum(total, axis=0, keepdims=True) / cells
            spread = 0.0
            for i in range(images):
                centred = jnp.where(inside, y[block_rows(i), :, lane] - mean, 0.0)
                spread = spread + jnp.sum(centred * centred, axis=0)
            mine[phase, k : k + 1, :] = mean
            mine[phase, chunks + k : chunks + k + 1, :] = jnp.sum(spread, axis=0, keepdims=True)

    def send_statistics(phase):
        def send(d, carry):
            peer = lax.rem(me + d, replicas)
            pltpu.make_async_remote_copy(
                src_ref=mine.at[phase],
                dst_ref=slots.at[phase, d - 1],
                send_sem=stat_send.at[phase],
                recv_sem=stat_recv.at[phase],
                device_id={"section": sec, "replica": peer},
                device_id_type=MESH,
            ).start()
            return carry

        lax.fori_loop(1, replicas, send, 0)

    def combine(phase, layer):
        pltpu.make_async_copy(slots.at[phase], slots.at[phase], stat_recv.at[phase]).wait()
        own = mine[phase]
        others = slots[phase]
        total = own + jnp.sum(others, axis=0)
        mean = total[0:chunks] / replicas
        apart = (own[0:chunks] - mean) ** 2 + jnp.sum(
            (others[:, 0:chunks] - mean[None]) ** 2, axis=0
        )
        var = (total[chunks:] + apart * cells) / (cells * replicas)
        scale = affine[layer, 0:chunks, :] * lax.rsqrt(var + 1e-05)
        coef[phase, 0:chunks, :] = scale
        coef[phase, chunks:, :] = affine[layer, chunks:, :] - mean * scale

    def activate(values, table, k):
        scale = table[k : k + 1, :]
        offset = table[chunks + k : chunks + k + 1, :]
        return jnp.maximum(values * scale[None] + offset[None], 0.0)

    def lay_hidden(phase):
        table = coef[phase]
        for k in range(chunks):
            lane = slice(k * LANES, (k + 1) * LANES)
            for i in range(images):
                lay(i, k, activate(y[block_rows(i), :, lane], table, k))

    def give_result(tick, phase):
        table = coef[phase]
        for k in range(chunks):
            lane = slice(k * LANES, (k + 1) * LANES)
            for i in range(images):
                done = activate(y[block_rows(i), 0:cols, lane], table, k)
                result[tick, i, :, :, lane] = done.astype(BF16)
        pltpu.make_async_copy(result.at[tick], out.at[0, tick], out_sem.at[tick]).start()

    map_copies[0].wait()
    lay_maps(0)
    for dy in range(3):
        weight_copies[0][dy].wait()
        for n in range(halves):
            multiply(0, n, [(dy, half) for half in range(halves)], dy > 0)
    gather_statistics(0)
    pl.semaphore_wait(
        barrier,
        replicas - 1 + (sec > 0).astype(jnp.int32) + (sec < sections - 1).astype(jnp.int32),
    )
    send_statistics(0)
    for dy in range(3):
        weight_copies[1][dy].wait()
    map_copies[1].wait()
    combine(0, 0)
    lay_hidden(0)

    def bulk(n):
        return pltpu.make_async_remote_copy(
            src_ref=sent.at[n],
            dst_ref=landed.at[n],
            send_sem=bulk_send.at[n],
            recv_sem=bulk_recv.at[n],
            device_id={"section": sec + 1, "replica": me},
            device_id_type=MESH,
        )

    def coefficients():
        return pltpu.make_async_remote_copy(
            src_ref=coef.at[1],
            dst_ref=moved_coef,
            send_sem=coef_send,
            recv_sem=coef_recv,
            device_id={"section": sec + 1, "replica": me},
            device_id_type=MESH,
        )

    for n in range(halves):
        multiply(1, n, every, False)
        lane = slice(n * TILE, (n + 1) * TILE)
        for i in range(images):
            sent[n, i] = y[block_rows(i), :, lane].astype(BF16)

        @pl.when(sec < sections - 1)
        def _():
            bulk(n).start()

    gather_statistics(1)
    send_statistics(1)
    combine(1, 1)

    @pl.when(sec < sections - 1)
    def _():
        coefficients().start()

    give_result(0, 1)

    @pl.when(sec == 0)
    def _():
        lay_maps(1)

    def lay_landed(half):
        bulk(half).wait_recv()
        table = moved_coef[...]
        for k in range(half * TILE // LANES, (half + 1) * TILE // LANES):
            at = k * LANES - half * TILE
            for i in range(images):
                values = landed[half, i, :, :, at : at + LANES].astype(F32)
                lay(i, k, activate(values, table, k))

    for half in range(halves):

        @pl.when(sec > 0)
        def _():
            if half == 0:
                coefficients().wait_recv()
            lay_landed(half)

        for n in range(halves):
            multiply(0, n, [(dy, half) for dy in range(3)], half > 0)
    gather_statistics(2)
    send_statistics(2)
    combine(2, 0)
    lay_hidden(2)

    for n in range(halves):
        multiply(1, n, every, False)
    gather_statistics(3)
    send_statistics(3)
    combine(3, 1)
    give_result(1, 3)

    for phase in range(4):
        pltpu.make_async_copy(slots.at[phase], slots.at[phase], stat_send.at[phase]).wait()

    @pl.when(sec < sections - 1)
    def _():
        for n in range(halves):
            bulk(n).wait_send()
        coefficients().wait_send()

    for tick in range(2):
        pltpu.make_async_copy(result.at[tick], out.at[0, tick], out_sem.at[tick]).wait()


def solution(mesh):
    sections, replicas = mesh.shape["section"], mesh.shape["replica"]

    def body(pend, arriving, first, second, gain, bias):
        images, rows, cols, channels = pend.shape[1:]
        blocks = images * (rows + 1) - 1
        halves = channels // TILE
        tile = 2 * channels // LANES
        dma = pltpu.SemaphoreType.DMA
        anywhere = pl.BlockSpec(memory_space=pl.ANY)
        vmem = pl.BlockSpec(memory_space=pltpu.VMEM)
        depth = 9 * channels * channels
        return pl.pallas_call(
            functools.partial(kernel, sections, replicas),
            out_shape=jax.ShapeDtypeStruct((1, 2, images, rows, cols, channels), BF16),
            in_specs=[anywhere] * 4 + [vmem] * 2,
            out_specs=anywhere,
            scratch_shapes=[
                pltpu.VMEM((2, images, rows, cols, channels), BF16),
                pltpu.VMEM((2, 3, 3, channels, channels), BF16),
                pltpu.VMEM((halves, (blocks + 2) * PITCH, 3 * TILE), BF16),
                pltpu.VMEM((blocks, PITCH, channels), F32),
                pltpu.VMEM((halves, images, rows, PITCH, TILE), BF16),
                pltpu.VMEM((halves, images, rows, PITCH, TILE), BF16),
                pltpu.VMEM((4, tile, LANES), F32),
                pltpu.VMEM((4, replicas - 1, tile, LANES), F32),
                pltpu.VMEM((4, tile, LANES), F32),
                pltpu.VMEM((tile, LANES), F32),
                pltpu.VMEM((2, tile, LANES), F32),
                pltpu.VMEM((2, images, rows, cols, channels), BF16),
                dma((2,)),
                dma((2, 3)),
                dma((2,)),
                dma((4,)),
                dma((4,)),
                dma((halves,)),
                dma((halves,)),
                dma,
                dma,
            ],
            compiler_params=pltpu.CompilerParams(
                collective_id=0, has_side_effects=True, vmem_limit_bytes=56 * 2**20
            ),
            cost_estimate=pl.CostEstimate(
                flops=8 * images * rows * cols * depth,
                bytes_accessed=4 * depth,
                transcendentals=0,
            ),
            name="relay",
        )(pend, arriving, first, second, gain, bias)

    in_specs = (
        P("section", "replica", None, None, None),
        P(None, "replica", None, None, None),
        P("section", None, None, None, None),
        P("section", None, None, None, None),
        P("section", None, None),
        P("section", None, None),
    )
    out_specs = P("section", None, "replica", None, None, None)
    return jax.shard_map(body, mesh=mesh, in_specs=in_specs, out_specs=out_specs, check_vma=False)
```

```python
import functools

import jax
import jax.numpy as jnp
from jax import lax
from jax.experimental import pallas as pl
from jax.experimental.pallas import tpu as pltpu
from jax.sharding import PartitionSpec as P

MESH = pl.DeviceIdType.MESH
F32 = jnp.float32
BF16 = jnp.bfloat16
LANES = 128
SLOTS = 16
TILE = 256


def kernel(
    sections,
    replicas,
    pend,
    arriving,
    first,
    second,
    gain,
    bias,
    out,
    maps,
    weights,
    taps,
    y,
    sent,
    landed,
    mine,
    slots,
    coef,
    moved_coef,
    affine,
    result,
    map_sem,
    weight_sem,
    out_sem,
    stat_send,
    stat_recv,
    bulk_send,
    bulk_recv,
    coef_send,
    coef_recv,
):
    rows, _, images, _ = maps.shape[2:]
    cols, channels = pend.shape[2], pend.shape[4]
    pitch = SLOTS * images
    chunks = channels // LANES
    halves = channels // TILE
    cells = images * rows * cols
    sec = lax.axis_index("section")
    me = lax.axis_index("replica")

    barrier = pltpu.get_barrier_semaphore()

    def greet(d, carry):
        peer = lax.rem(me + d, replicas)
        pl.semaphore_signal(
            barrier, inc=1, device_id={"section": sec, "replica": peer}, device_id_type=MESH
        )
        return carry

    lax.fori_loop(1, replicas, greet, 0)

    @pl.when(sec > 0)
    def _():
        pl.semaphore_signal(
            barrier, inc=1, device_id={"section": sec - 1, "replica": me}, device_id_type=MESH
        )

    @pl.when(sec < sections - 1)
    def _():
        pl.semaphore_signal(
            barrier, inc=1, device_id={"section": sec + 1, "replica": me}, device_id_type=MESH
        )

    def lanes(k):
        return slice(k * LANES, (k + 1) * LANES)

    map_copies = [
        [
            pltpu.make_async_copy(
                src.at[0, :, :, :, pl.ds(k * LANES, LANES)],
                maps.at[which, k, :, pl.ds(0, cols)],
                map_sem.at[which, k],
            )
            for k in range(chunks)
        ]
        for which, src in enumerate((pend, arriving))
    ]
    out_copies = [
        [
            pltpu.make_async_copy(
                result.at[tick, k, :, pl.ds(0, cols)],
                out.at[0, tick, :, :, :, pl.ds(k * LANES, LANES)],
                out_sem.at[tick, k],
            )
            for k in range(chunks)
        ]
        for tick in range(2)
    ]
    flat_maps = maps.reshape(2, chunks, rows * pitch, LANES)
    flat_result = result.reshape(2, chunks, rows * pitch, LANES)
    weight_copies = [
        [
            pltpu.make_async_copy(src.at[0, dy], weights.at[layer, dy], weight_sem.at[layer, dy])
            for dy in range(3)
        ]
        for layer, src in enumerate((first, second))
    ]
    for copy in map_copies[0]:
        copy.start()
    for layer in range(2):
        for dy in range(3):
            weight_copies[layer][dy].start()
    for copy in map_copies[1]:
        copy.start()

    for layer in range(2):
        for k in range(chunks):
            lane = slice(k * LANES, (k + 1) * LANES)
            affine[layer, k : k + 1, :] = gain[0, layer : layer + 1, lane]
            affine[layer, chunks + k : chunks + k + 1, :] = bias[0, layer : layer + 1, lane]

    pad = jnp.zeros((halves, pitch, 3 * TILE), BF16)
    taps[:, 0:pitch, :] = pad
    taps[:, (rows + 1) * pitch : (rows + 2) * pitch, :] = pad

    inside = (
        lax.broadcasted_iota(jnp.int32, (rows, pitch, LANES), 1).reshape(rows * pitch, LANES)
        < cols * images
    )

    def lay(k, values):
        flat = jnp.where(inside, values, 0.0)
        half, lane = (k * LANES) // TILE, (k * LANES) % TILE
        where = slice(pitch, (rows + 1) * pitch)
        taps[half, where, lane : lane + LANES] = pltpu.roll(flat, images, 0).astype(BF16)
        taps[half, where, TILE + lane : TILE + lane + LANES] = flat.astype(BF16)
        taps[half, where, 2 * TILE + lane : 2 * TILE + lane + LANES] = pltpu.roll(
            flat, rows * pitch - images, 0
        ).astype(BF16)

    def lay_maps(which):
        for k in range(chunks):
            lay(k, flat_maps[which, k].astype(F32))

    def multiply(layer, parts, add):
        total = None
        for dy, half in parts:
            left = taps[half, dy * pitch : (dy + rows) * pitch, :]
            right = weights[layer, dy, :, half * TILE : (half + 1) * TILE, :]
            term = jnp.dot(
                left, right.reshape(3 * TILE, channels), preferred_element_type=F32
            )
            total = term if total is None else total + term
        y[...] = y[...] + total if add else total

    every = [(dy, half) for half in range(halves) for dy in range(3)]

    def gather_statistics(phase):
        for k in range(chunks):
            total = jnp.sum(jnp.where(inside, y[:, lanes(k)], 0.0), axis=0, keepdims=True)
            mean = total / cells
            centred = jnp.where(inside, y[:, lanes(k)] - mean, 0.0)
            mine[phase, k : k + 1, :] = mean
            mine[phase, chunks + k : chunks + k + 1, :] = jnp.sum(
                centred * centred, axis=0, keepdims=True
            )

    def send_statistics(phase):
        def send(d, carry):
            peer = lax.rem(me + d, replicas)
            pltpu.make_async_remote_copy(
                src_ref=mine.at[phase],
                dst_ref=slots.at[phase, d - 1],
                send_sem=stat_send.at[phase],
                recv_sem=stat_recv.at[phase],
                device_id={"section": sec, "replica": peer},
                device_id_type=MESH,
            ).start()
            return carry

        lax.fori_loop(1, replicas, send, 0)

    def combine(phase, layer):
        pltpu.make_async_copy(slots.at[phase], slots.at[phase], stat_recv.at[phase]).wait()
        own = mine[phase]
        others = slots[phase]
        total = own + jnp.sum(others, axis=0)
        mean = total[0:chunks] / replicas
        apart = (own[0:chunks] - mean) ** 2 + jnp.sum(
            (others[:, 0:chunks] - mean[None]) ** 2, axis=0
        )
        var = (total[chunks:] + apart * cells) / (cells * replicas)
        scale = affine[layer, 0:chunks, :] * lax.rsqrt(var + 1e-05)
        coef[phase, 0:chunks, :] = scale
        coef[phase, chunks:, :] = affine[layer, chunks:, :] - mean * scale

    def activate(values, table, k):
        scale = table[k : k + 1, :]
        offset = table[chunks + k : chunks + k + 1, :]
        return jnp.maximum(values * scale + offset, 0.0)

    def lay_hidden(phase):
        table = coef[phase]
        for k in range(chunks):
            lay(k, activate(y[:, lanes(k)], table, k))

    def give_result(tick, phase):
        table = coef[phase]
        for k in range(chunks):
            flat_result[tick, k] = activate(y[:, lanes(k)], table, k).astype(BF16)
            out_copies[tick][k].start()

    for copy in map_copies[0]:
        copy.wait()
    lay_maps(0)
    for dy in range(3):
        weight_copies[0][dy].wait()
        multiply(0, [(dy, half) for half in range(halves)], dy > 0)
    gather_statistics(0)
    pl.semaphore_wait(
        barrier,
        replicas - 1 + (sec > 0).astype(jnp.int32) + (sec < sections - 1).astype(jnp.int32),
    )
    send_statistics(0)
    for dy in range(3):
        weight_copies[1][dy].wait()
    for copy in map_copies[1]:
        copy.wait()
    combine(0, 0)
    lay_hidden(0)

    def bulk(n):
        return pltpu.make_async_remote_copy(
            src_ref=sent.at[n],
            dst_ref=landed.at[n],
            send_sem=bulk_send.at[n],
            recv_sem=bulk_recv.at[n],
            device_id={"section": sec + 1, "replica": me},
            device_id_type=MESH,
        )

    def coefficients():
        return pltpu.make_async_remote_copy(
            src_ref=coef.at[1],
            dst_ref=moved_coef,
            send_sem=coef_send,
            recv_sem=coef_recv,
            device_id={"section": sec + 1, "replica": me},
            device_id_type=MESH,
        )

    multiply(1, every, False)
    for n in range(halves):
        sent[n] = y[:, n * TILE : (n + 1) * TILE].astype(BF16)

        @pl.when(sec < sections - 1)
        def _():
            bulk(n).start()

    gather_statistics(1)
    send_statistics(1)
    combine(1, 1)

    @pl.when(sec < sections - 1)
    def _():
        coefficients().start()

    give_result(0, 1)

    @pl.when(sec == 0)
    def _():
        lay_maps(1)

    def lay_landed(half):
        bulk(half).wait_recv()
        table = moved_coef[...]
        for k in range(half * TILE // LANES, (half + 1) * TILE // LANES):
            at = k * LANES - half * TILE
            values = landed[half, :, at : at + LANES].astype(F32)
            lay(k, activate(values, table, k))

    for half in range(halves):

        @pl.when(sec > 0)
        def _():
            if half == 0:
                coefficients().wait_recv()
            lay_landed(half)

        multiply(0, [(dy, half) for dy in range(3)], half > 0)
    gather_statistics(2)
    send_statistics(2)
    combine(2, 0)
    lay_hidden(2)

    multiply(1, every, False)
    gather_statistics(3)
    send_statistics(3)
    combine(3, 1)
    give_result(1, 3)

    for phase in range(4):
        pltpu.make_async_copy(slots.at[phase], slots.at[phase], stat_send.at[phase]).wait()

    @pl.when(sec < sections - 1)
    def _():
        for n in range(halves):
            bulk(n).wait_send()
        coefficients().wait_send()

    for copies in out_copies:
        for copy in copies:
            copy.wait()


def solution(mesh):
    sections, replicas = mesh.shape["section"], mesh.shape["replica"]

    def body(pend, arriving, first, second, gain, bias):
        images, rows, cols, channels = pend.shape[1:]
        pend = jnp.transpose(pend, (0, 2, 3, 1, 4))
        arriving = jnp.transpose(arriving, (0, 2, 3, 1, 4))
        pitch = SLOTS * images
        chunks = channels // LANES
        halves = channels // TILE
        tile = 2 * channels // LANES
        dma = pltpu.SemaphoreType.DMA
        anywhere = pl.BlockSpec(memory_space=pl.ANY)
        vmem = pl.BlockSpec(memory_space=pltpu.VMEM)
        depth = 9 * channels * channels
        produced = pl.pallas_call(
            functools.partial(kernel, sections, replicas),
            out_shape=jax.ShapeDtypeStruct((1, 2, rows, cols, images, channels), BF16),
            in_specs=[anywhere] * 4 + [vmem] * 2,
            out_specs=anywhere,
            scratch_shapes=[
                pltpu.VMEM((2, chunks, rows, SLOTS, images, LANES), BF16),
                pltpu.VMEM((2, 3, 3, channels, channels), BF16),
                pltpu.VMEM((halves, (rows + 2) * pitch, 3 * TILE), BF16),
                pltpu.VMEM((rows * pitch, channels), F32),
                pltpu.VMEM((halves, rows * pitch, TILE), BF16),
                pltpu.VMEM((halves, rows * pitch, TILE), BF16),
                pltpu.VMEM((4, tile, LANES), F32),
                pltpu.VMEM((4, replicas - 1, tile, LANES), F32),
                pltpu.VMEM((4, tile, LANES), F32),
                pltpu.VMEM((tile, LANES), F32),
                pltpu.VMEM((2, tile, LANES), F32),
                pltpu.VMEM((2, chunks, rows, SLOTS, images, LANES), BF16),
                dma((2, chunks)),
                dma((2, 3)),
                dma((2, chunks)),
                dma((4,)),
                dma((4,)),
                dma((halves,)),
                dma((halves,)),
                dma,
                dma,
            ],
            compiler_params=pltpu.CompilerParams(
                collective_id=0, has_side_effects=True, vmem_limit_bytes=56 * 2**20
            ),
            cost_estimate=pl.CostEstimate(
                flops=8 * images * rows * cols * depth,
                bytes_accessed=4 * depth,
                transcendentals=0,
            ),
            name="relay",
        )(pend, arriving, first, second, gain, bias)
        return jnp.transpose(produced, (0, 1, 4, 2, 3, 5))

    in_specs = (
        P("section", "replica", None, None, None),
        P(None, "replica", None, None, None),
        P("section", None, None, None, None),
        P("section", None, None, None, None),
        P("section", None, None),
        P("section", None, None),
    )
    out_specs = P("section", None, "replica", None, None, None)
    return jax.shard_map(body, mesh=mesh, in_specs=in_specs, out_specs=out_specs, check_vma=False)
```

```python
import functools

import jax
import jax.numpy as jnp
from jax import lax
from jax.experimental import pallas as pl
from jax.experimental.pallas import tpu as pltpu
from jax.sharding import PartitionSpec as P

MESH = pl.DeviceIdType.MESH
F32 = jnp.float32
BF16 = jnp.bfloat16
LANES = 128
SLOTS = 16
TILE = 256


def kernel(
    sections,
    replicas,
    pend,
    arriving,
    first,
    second,
    gain,
    bias,
    out,
    maps,
    weights,
    taps,
    y,
    sent,
    landed,
    mine,
    slots,
    coef,
    moved_coef,
    affine,
    result,
    map_sem,
    weight_sem,
    out_sem,
    stat_send,
    stat_recv,
    bulk_send,
    bulk_recv,
    coef_send,
    coef_recv,
):
    rows, _, images, _ = maps.shape[2:]
    cols, channels = pend.shape[2], pend.shape[4]
    pitch = SLOTS * images
    chunks = channels // LANES
    halves = channels // TILE
    per = TILE // LANES
    cells = images * rows * cols
    sec = lax.axis_index("section")
    me = lax.axis_index("replica")

    barrier = pltpu.get_barrier_semaphore()

    def greet(d, carry):
        peer = lax.rem(me + d, replicas)
        pl.semaphore_signal(
            barrier, inc=1, device_id={"section": sec, "replica": peer}, device_id_type=MESH
        )
        return carry

    lax.fori_loop(1, replicas, greet, 0)

    @pl.when(sec > 0)
    def _():
        pl.semaphore_signal(
            barrier, inc=1, device_id={"section": sec - 1, "replica": me}, device_id_type=MESH
        )

    @pl.when(sec < sections - 1)
    def _():
        pl.semaphore_signal(
            barrier, inc=1, device_id={"section": sec + 1, "replica": me}, device_id_type=MESH
        )

    def lanes(k):
        return slice(k * LANES, (k + 1) * LANES)

    map_copies = [
        [
            pltpu.make_async_copy(
                src.at[0, :, :, :, pl.ds(k * LANES, LANES)],
                maps.at[which, k, :, pl.ds(0, cols)],
                map_sem.at[which, k],
            )
            for k in range(chunks)
        ]
        for which, src in enumerate((pend, arriving))
    ]
    out_copies = [
        [
            pltpu.make_async_copy(
                result.at[tick, k, :, pl.ds(0, cols)],
                out.at[0, tick, :, :, :, pl.ds(k * LANES, LANES)],
                out_sem.at[tick, k],
            )
            for k in range(chunks)
        ]
        for tick in range(2)
    ]
    flat_maps = maps.reshape(2, chunks, rows * pitch, LANES)
    flat_result = result.reshape(2, chunks, rows * pitch, LANES)
    flat_sent = sent.reshape(chunks, rows * pitch, LANES)
    flat_landed = landed.reshape(chunks, rows * pitch, LANES)
    weight_copies = [
        [
            pltpu.make_async_copy(src.at[0, dy], weights.at[layer, dy], weight_sem.at[layer, dy])
            for dy in range(3)
        ]
        for layer, src in enumerate((first, second))
    ]
    for copy in map_copies[0]:
        copy.start()
    for layer in range(2):
        for dy in range(3):
            weight_copies[layer][dy].start()
    for copy in map_copies[1]:
        copy.start()

    for layer in range(2):
        for k in range(chunks):
            lane = slice(k * LANES, (k + 1) * LANES)
            g, j = divmod(k, per)
            affine[layer, g, j : j + 1, :] = gain[0, layer : layer + 1, lane]
            affine[layer, g, per + j : per + j + 1, :] = bias[0, layer : layer + 1, lane]

    pad = jnp.zeros((halves, pitch, 3 * TILE), BF16)
    taps[:, 0:pitch, :] = pad
    taps[:, (rows + 1) * pitch : (rows + 2) * pitch, :] = pad

    inside = (
        lax.broadcasted_iota(jnp.int32, (rows, pitch, LANES), 1).reshape(rows * pitch, LANES)
        < cols * images
    )

    def lay(k, values):
        flat = jnp.where(inside, values, 0.0)
        half, lane = (k * LANES) // TILE, (k * LANES) % TILE
        where = slice(pitch, (rows + 1) * pitch)
        taps[half, where, lane : lane + LANES] = pltpu.roll(flat, images, 0).astype(BF16)
        taps[half, where, TILE + lane : TILE + lane + LANES] = flat.astype(BF16)
        taps[half, where, 2 * TILE + lane : 2 * TILE + lane + LANES] = pltpu.roll(
            flat, rows * pitch - images, 0
        ).astype(BF16)

    def lay_maps(which):
        for k in range(chunks):
            lay(k, flat_maps[which, k].astype(F32))

    def multiply(which, layer, parts, group, add):
        lane = slice(0, channels) if group is None else slice(group * TILE, (group + 1) * TILE)
        total = None
        for dy, half in parts:
            left = taps[half, dy * pitch : (dy + rows) * pitch, :]
            right = weights[layer, dy, :, half * TILE : (half + 1) * TILE, lane]
            term = jnp.dot(
                left,
                right.reshape(3 * TILE, lane.stop - lane.start),
                preferred_element_type=F32,
            )
            total = term if total is None else total + term
        y[which, :, lane] = y[which, :, lane] + total if add else total

    def taps_of(half):
        return [(dy, half) for dy in range(3)]

    def send_statistics(which, phase, g):
        for j in range(per):
            lane = lanes(g * per + j)
            total = jnp.sum(jnp.where(inside, y[which, :, lane], 0.0), axis=0, keepdims=True)
            mean = total / cells
            centred = jnp.where(inside, y[which, :, lane] - mean, 0.0)
            mine[phase, g, j : j + 1, :] = mean
            mine[phase, g, per + j : per + j + 1, :] = jnp.sum(
                centred * centred, axis=0, keepdims=True
            )

        def send(d, carry):
            peer = lax.rem(me + d, replicas)
            pltpu.make_async_remote_copy(
                src_ref=mine.at[phase, g],
                dst_ref=slots.at[phase, g, d - 1],
                send_sem=stat_send.at[phase, g],
                recv_sem=stat_recv.at[phase, g],
                device_id={"section": sec, "replica": peer},
                device_id_type=MESH,
            ).start()
            return carry

        lax.fori_loop(1, replicas, send, 0, unroll=replicas <= 16)

    def combine(phase, layer, g):
        here = slots.at[phase, g]
        pltpu.make_async_copy(here, here, stat_recv.at[phase, g]).wait()
        own = mine[phase, g]
        others = slots[phase, g]
        total = own + jnp.sum(others, axis=0)
        mean = total[0:per] / replicas
        apart = (own[0:per] - mean) ** 2 + jnp.sum((others[:, 0:per] - mean[None]) ** 2, axis=0)
        var = (total[per:] + apart * cells) / (cells * replicas)
        scale = affine[layer, g, 0:per, :] * lax.rsqrt(var + 1e-05)
        coef[phase, g, 0:per, :] = scale
        coef[phase, g, per:, :] = affine[layer, g, per:, :] - mean * scale

    def activate(values, table, j):
        return jnp.maximum(values * table[j : j + 1, :] + table[per + j : per + j + 1, :], 0.0)

    def lay_hidden(which, phase, g):
        table = coef[phase, g]
        for j in range(per):
            k = g * per + j
            lay(k, activate(y[which, :, lanes(k)], table, j))

    def give_result(which, tick, phase, g):
        table = coef[phase, g]
        for j in range(per):
            k = g * per + j
            flat_result[tick, k] = activate(y[which, :, lanes(k)], table, j).astype(BF16)
            out_copies[tick][k].start()

    def bulk(k):
        return pltpu.make_async_remote_copy(
            src_ref=sent.at[k, :, pl.ds(0, cols)],
            dst_ref=landed.at[k, :, pl.ds(0, cols)],
            send_sem=bulk_send.at[k],
            recv_sem=bulk_recv.at[k],
            device_id={"section": sec + 1, "replica": me},
            device_id_type=MESH,
        )

    def coefficients(g):
        return pltpu.make_async_remote_copy(
            src_ref=coef.at[1, g],
            dst_ref=moved_coef.at[g],
            send_sem=coef_send.at[g],
            recv_sem=coef_recv.at[g],
            device_id={"section": sec + 1, "replica": me},
            device_id_type=MESH,
        )

    has_next = sec < sections - 1
    has_previous = sec > 0

    for copy in map_copies[0]:
        copy.wait()
    lay_maps(0)
    for dy in range(3):
        weight_copies[0][dy].wait()
        parts = [(dy, half) for half in range(halves)]
        if dy < 2:
            multiply(0, 0, parts, None, dy > 0)
    for g in range(halves):
        multiply(0, 0, parts, g, True)
        if g == 0:
            pl.semaphore_wait(
                barrier,
                replicas - 1 + has_previous.astype(jnp.int32) + has_next.astype(jnp.int32),
            )
        send_statistics(0, 0, g)
    for dy in range(3):
        weight_copies[1][dy].wait()
    for copy in map_copies[1]:
        copy.wait()

    for half in range(halves):
        combine(0, 0, half)
        lay_hidden(0, 0, half)
        multiply(1, 1, taps_of(half), 0, half > 0)
    for g in range(halves):
        if g > 0:
            for half in range(halves):
                multiply(1, 1, taps_of(half), g, half > 0)
        for j in range(per):
            k = g * per + j
            flat_sent[k] = y[1, :, lanes(k)].astype(BF16)

        @pl.when(has_next)
        def _():
            for k in range(g * per, (g + 1) * per):
                if k < chunks - 1:
                    bulk(k).start()

        send_statistics(1, 1, g)
    for g in range(halves):
        combine(1, 1, g)

        @pl.when(has_next)
        def _():
            coefficients(g).start()
            if g == 0:
                bulk(chunks - 1).start()

    for g in range(halves):
        give_result(1, 0, 1, g)

    @pl.when(sec == 0)
    def _():
        lay_maps(1)

    for half in range(halves):

        @pl.when(has_previous)
        def _():
            coefficients(half).wait_recv()
            table = moved_coef[half]
            for j in range(per):
                k = half * per + j
                bulk(k).wait_recv()
                lay(k, activate(flat_landed[k].astype(F32), table, j))

        if half < halves - 1:
            multiply(0, 0, taps_of(half), None, half > 0)
    for g in range(halves):
        multiply(0, 0, taps_of(halves - 1), g, halves > 1)
        send_statistics(0, 2, g)

    for half in range(halves):
        combine(2, 0, half)
        lay_hidden(0, 2, half)
        if half < halves - 1:
            multiply(1, 1, taps_of(half), None, half > 0)
    for g in range(halves):
        multiply(1, 1, taps_of(halves - 1), g, halves > 1)
        send_statistics(1, 3, g)
    for g in range(halves):
        combine(3, 1, g)
        give_result(1, 1, 3, g)

    for phase in range(4):
        for g in range(halves):
            here = slots.at[phase, g]
            pltpu.make_async_copy(here, here, stat_send.at[phase, g]).wait()

    @pl.when(has_next)
    def _():
        for k in range(chunks):
            bulk(k).wait_send()
        for g in range(halves):
            coefficients(g).wait_send()

    for copies in out_copies:
        for copy in copies:
            copy.wait()


def hand_over(given, out, sems):
    ticks, rows = given.shape[1:3]
    cut = (rows + 1) // 2
    copies = []
    for tick in range(ticks):
        for n, part in enumerate((pl.ds(0, cut), pl.ds(cut, rows - cut))):
            copies.append(
                pltpu.make_async_copy(
                    given.at[0, tick, part], out.at[0, tick, part], sems.at[tick, n]
                )
            )
    for copy in copies:
        copy.start()
    for copy in copies:
        copy.wait()


def solution(mesh):
    sections, replicas = mesh.shape["section"], mesh.shape["replica"]

    def body(pend, arriving, first, second, gain, bias):
        images, rows, cols, channels = pend.shape[1:]
        pend = jnp.transpose(pend, (0, 2, 3, 1, 4))
        arriving = jnp.transpose(arriving, (0, 2, 3, 1, 4))
        pitch = SLOTS * images
        chunks = channels // LANES
        halves = channels // TILE
        tile = 2 * TILE // LANES
        limit = 56 * 2**20
        dma = pltpu.SemaphoreType.DMA
        anywhere = pl.BlockSpec(memory_space=pl.ANY)
        vmem = pl.BlockSpec(memory_space=pltpu.VMEM)
        depth = 9 * channels * channels
        produced = pl.pallas_call(
            functools.partial(kernel, sections, replicas),
            out_shape=jax.ShapeDtypeStruct((1, 2, rows, cols, images, channels), BF16),
            in_specs=[anywhere] * 4 + [vmem] * 2,
            out_specs=anywhere,
            scratch_shapes=[
                pltpu.VMEM((2, chunks, rows, SLOTS, images, LANES), BF16),
                pltpu.VMEM((2, 3, 3, channels, channels), BF16),
                pltpu.VMEM((halves, (rows + 2) * pitch, 3 * TILE), BF16),
                pltpu.VMEM((2, rows * pitch, channels), F32),
                pltpu.VMEM((chunks, rows, SLOTS, images, LANES), BF16),
                pltpu.VMEM((chunks, rows, SLOTS, images, LANES), BF16),
                pltpu.VMEM((4, halves, tile, LANES), F32),
                pltpu.VMEM((4, halves, replicas - 1, tile, LANES), F32),
                pltpu.VMEM((4, halves, tile, LANES), F32),
                pltpu.VMEM((halves, tile, LANES), F32),
                pltpu.VMEM((2, halves, tile, LANES), F32),
                pltpu.VMEM((2, chunks, rows, SLOTS, images, LANES), BF16),
                dma((2, chunks)),
                dma((2, 3)),
                dma((2, chunks)),
                dma((4, halves)),
                dma((4, halves)),
                dma((chunks,)),
                dma((chunks,)),
                dma((halves,)),
                dma((halves,)),
            ],
            compiler_params=pltpu.CompilerParams(
                collective_id=0, has_side_effects=True, vmem_limit_bytes=limit
            ),
            cost_estimate=pl.CostEstimate(
                flops=8 * images * rows * cols * depth,
                bytes_accessed=4 * depth,
                transcendentals=0,
            ),
            name="relay",
        )(pend, arriving, first, second, gain, bias)
        produced = pl.pallas_call(
            hand_over,
            out_shape=jax.ShapeDtypeStruct(produced.shape, BF16),
            in_specs=[anywhere],
            out_specs=anywhere,
            scratch_shapes=[dma((2, 2))],
            compiler_params=pltpu.CompilerParams(vmem_limit_bytes=limit),
            name="hand_over",
        )(produced)
        return jnp.transpose(produced, (0, 1, 4, 2, 3, 5))

    in_specs = (
        P("section", "replica", None, None, None),
        P(None, "replica", None, None, None),
        P("section", None, None, None, None),
        P("section", None, None, None, None),
        P("section", None, None),
        P("section", None, None),
    )
    out_specs = P("section", None, "replica", None, None, None)
    return jax.shard_map(body, mesh=mesh, in_specs=in_specs, out_specs=out_specs, check_vma=False)
```

```python
import functools

import jax
import jax.numpy as jnp
from jax import lax
from jax.experimental import pallas as pl
from jax.experimental.pallas import tpu as pltpu
from jax.sharding import PartitionSpec as P

MESH = pl.DeviceIdType.MESH
F32 = jnp.float32
BF16 = jnp.bfloat16
LANES = 128
SLOTS = 16
TILE = 256


def kernel(
    sections,
    replicas,
    pend,
    arriving,
    first,
    second,
    gain,
    bias,
    out,
    maps,
    weights,
    taps,
    y,
    sent,
    landed,
    mine,
    slots,
    coef,
    moved_coef,
    affine,
    result,
    map_sem,
    weight_sem,
    out_sem,
    stat_send,
    stat_recv,
    bulk_send,
    bulk_recv,
    coef_send,
    coef_recv,
):
    rows, _, images, _ = maps.shape[2:]
    cols, channels = pend.shape[2], pend.shape[4]
    pitch = SLOTS * images
    chunks = channels // LANES
    halves = channels // TILE
    per = TILE // LANES
    cells = images * rows * cols
    sec = lax.axis_index("section")
    me = lax.axis_index("replica")

    barrier = pltpu.get_barrier_semaphore()

    def greet(d, carry):
        peer = lax.rem(me + d, replicas)
        pl.semaphore_signal(
            barrier, inc=1, device_id={"section": sec, "replica": peer}, device_id_type=MESH
        )
        return carry

    lax.fori_loop(1, replicas, greet, 0)

    @pl.when(sec > 0)
    def _():
        pl.semaphore_signal(
            barrier, inc=1, device_id={"section": sec - 1, "replica": me}, device_id_type=MESH
        )

    @pl.when(sec < sections - 1)
    def _():
        pl.semaphore_signal(
            barrier, inc=1, device_id={"section": sec + 1, "replica": me}, device_id_type=MESH
        )

    def lanes(k):
        return pl.ds(pl.multiple_of(k * LANES, LANES), LANES)

    def each(count, step):
        lax.fori_loop(0, count, lambda i, carry: step(i), None)

    map_copies = [
        [
            pltpu.make_async_copy(
                src.at[0, :, :, :, pl.ds(k * LANES, LANES)],
                maps.at[which, k, :, pl.ds(0, cols)],
                map_sem.at[which, k],
            )
            for k in range(chunks)
        ]
        for which, src in enumerate((pend, arriving))
    ]
    out_copies = [
        [
            pltpu.make_async_copy(
                result.at[tick, k, :, pl.ds(0, cols)],
                out.at[0, tick, :, :, :, pl.ds(k * LANES, LANES)],
                out_sem.at[tick, k],
            )
            for k in range(chunks)
        ]
        for tick in range(2)
    ]
    flat_maps = maps.reshape(2, chunks, rows * pitch, LANES)
    flat_result = result.reshape(2, chunks, rows * pitch, LANES)
    flat_sent = sent.reshape(chunks, rows * pitch, LANES)
    flat_landed = landed.reshape(chunks, rows * pitch, LANES)
    weight_copies = [
        [
            pltpu.make_async_copy(src.at[0, dy], weights.at[layer, dy], weight_sem.at[layer, dy])
            for dy in range(3)
        ]
        for layer, src in enumerate((first, second))
    ]
    for copy in map_copies[0]:
        copy.start()
    for layer in range(2):
        for dy in range(3):
            weight_copies[layer][dy].start()
    for copy in map_copies[1]:
        copy.start()

    for layer in range(2):
        for k in range(chunks):
            lane = slice(k * LANES, (k + 1) * LANES)
            affine[layer, k : k + 1, :] = gain[0, layer : layer + 1, lane]
            affine[layer, chunks + k : chunks + k + 1, :] = bias[0, layer : layer + 1, lane]

    pad = jnp.zeros((halves, pitch, 3 * TILE), BF16)
    taps[:, 0:pitch, :] = pad
    taps[:, (rows + 1) * pitch : (rows + 2) * pitch, :] = pad

    inside = (
        lax.broadcasted_iota(jnp.int32, (rows, pitch, LANES), 1).reshape(rows * pitch, LANES)
        < cols * images
    )

    def lay(k, values):
        flat = jnp.where(inside, values, 0.0)
        half, lane = k // per, (k % per) * LANES
        shifted = (pltpu.roll(flat, images, 0), flat, pltpu.roll(flat, rows * pitch - images, 0))
        for dx, tap in enumerate(shifted):
            at = pl.multiple_of(dx * TILE + lane, LANES)
            taps[half, pitch : (rows + 1) * pitch, pl.ds(at, LANES)] = tap.astype(BF16)

    def lay_maps(which):
        each(chunks, lambda k: lay(k, flat_maps[which, k].astype(F32)))

    def product(layer, dy, half, lane, width):
        left = taps[half, pl.ds(pl.multiple_of(dy * pitch, pitch), rows * pitch), :]
        right = weights[layer, dy, :, half * TILE : (half + 1) * TILE, lane : lane + width]
        return jnp.dot(left, right.reshape(3 * TILE, width), preferred_element_type=F32)

    def multiply(layer, parts, lane=0, width=channels, add=False, ready=None):
        where = slice(lane, lane + width)
        if not add:
            y[:, where] = jnp.zeros((rows * pitch, width), F32)

        def step(dy):
            if ready is not None:
                ready(dy)
            total = y[:, where]
            for half in parts:
                total = total + product(layer, dy, half, lane, width)
            y[:, where] = total

        each(3, step)

    everything = range(halves)

    def send_statistics(phase):
        def measure(k):
            total = jnp.sum(jnp.where(inside, y[:, lanes(k)], 0.0), axis=0, keepdims=True)
            mean = total / cells
            centred = jnp.where(inside, y[:, lanes(k)] - mean, 0.0)
            mine[phase, pl.ds(k, 1), :] = mean
            mine[phase, pl.ds(chunks + k, 1), :] = jnp.sum(
                centred * centred, axis=0, keepdims=True
            )

        each(chunks, measure)
        if phase == 0:
            pl.semaphore_wait(
                barrier,
                replicas - 1 + has_previous.astype(jnp.int32) + has_next.astype(jnp.int32),
            )

        def send(d, carry):
            peer = lax.rem(me + d, replicas)
            pltpu.make_async_remote_copy(
                src_ref=mine.at[phase],
                dst_ref=slots.at[phase, d - 1],
                send_sem=stat_send.at[phase],
                recv_sem=stat_recv.at[phase],
                device_id={"section": sec, "replica": peer},
                device_id_type=MESH,
            ).start()
            return carry

        lax.fori_loop(1, replicas, send, 0)

    def combine(phase, layer):
        here = slots.at[phase]
        pltpu.make_async_copy(here, here, stat_recv.at[phase]).wait()
        own = mine[phase]
        others = slots[phase]
        total = own + jnp.sum(others, axis=0)
        mean = total[0:chunks] / replicas
        apart = (own[0:chunks] - mean) ** 2 + jnp.sum(
            (others[:, 0:chunks] - mean[None]) ** 2, axis=0
        )
        var = (total[chunks:] + apart * cells) / (cells * replicas)
        scale = affine[layer, 0:chunks, :] * lax.rsqrt(var + 1e-05)
        coef[phase, 0:chunks, :] = scale
        coef[phase, chunks:, :] = affine[layer, chunks:, :] - mean * scale

    def activate(values, table, k):
        scale = table[pl.ds(k, 1), :]
        offset = table[pl.ds(chunks + k, 1), :]
        return jnp.maximum(values * scale + offset, 0.0)

    def lay_hidden(phase):
        each(chunks, lambda k: lay(k, activate(y[:, lanes(k)], coef.at[phase], k)))

    def give_result(tick, phase):
        def give(k):
            flat_result[tick, k] = activate(y[:, lanes(k)], coef.at[phase], k).astype(BF16)

        each(chunks, give)
        for copy in out_copies[tick]:
            copy.start()

    def bulk(k):
        return pltpu.make_async_remote_copy(
            src_ref=sent.at[k, :, pl.ds(0, cols)],
            dst_ref=landed.at[k, :, pl.ds(0, cols)],
            send_sem=bulk_send.at[k],
            recv_sem=bulk_recv.at[k],
            device_id={"section": sec + 1, "replica": me},
            device_id_type=MESH,
        )

    def coefficients():
        return pltpu.make_async_remote_copy(
            src_ref=coef.at[1],
            dst_ref=moved_coef,
            send_sem=coef_send,
            recv_sem=coef_recv,
            device_id={"section": sec + 1, "replica": me},
            device_id_type=MESH,
        )

    has_next = sec < sections - 1
    has_previous = sec > 0

    for copy in map_copies[0]:
        copy.wait()
    lay_maps(0)
    multiply(
        0,
        everything,
        ready=lambda dy: pltpu.make_async_copy(
            first.at[0, dy], weights.at[0, dy], weight_sem.at[0, dy]
        ).wait(),
    )
    send_statistics(0)
    for dy in range(3):
        weight_copies[1][dy].wait()
    for copy in map_copies[1]:
        copy.wait()
    combine(0, 0)
    lay_hidden(0)

    for g in range(halves):
        multiply(1, everything, g * TILE, TILE)
        for k in range(g * per, (g + 1) * per):
            flat_sent[k] = y[:, k * LANES : (k + 1) * LANES].astype(BF16)

        @pl.when(has_next)
        def _():
            for k in range(g * per, (g + 1) * per):
                if k < chunks - 1:
                    bulk(k).start()

    send_statistics(1)
    combine(1, 1)

    @pl.when(has_next)
    def _():
        coefficients().start()
        bulk(chunks - 1).start()

    give_result(0, 1)

    @pl.when(sec == 0)
    def _():
        lay_maps(1)

    for half in range(halves):

        @pl.when(has_previous)
        def _():
            if half == 0:
                coefficients().wait_recv()
            for k in range(half * per, (half + 1) * per):
                bulk(k).wait_recv()
                lay(k, activate(flat_landed[k].astype(F32), moved_coef, k))

        multiply(0, [half], add=half > 0)
    send_statistics(2)
    combine(2, 0)
    lay_hidden(2)

    multiply(1, everything)
    send_statistics(3)
    combine(3, 1)
    give_result(1, 3)

    for phase in range(4):
        here = slots.at[phase]
        pltpu.make_async_copy(here, here, stat_send.at[phase]).wait()

    @pl.when(has_next)
    def _():
        for k in range(chunks):
            bulk(k).wait_send()
        coefficients().wait_send()

    for copies in out_copies:
        for copy in copies:
            copy.wait()


def hand_over(given, out, held, in_sems, out_sems):
    ticks, rows = given.shape[1:3]
    cut = (rows + 1) // 2
    parts = [(t, p) for t in range(ticks) for p in (pl.ds(0, cut), pl.ds(cut, rows - cut))]
    fetch, give = [], []
    for n, (t, part) in enumerate(parts):
        here = held.at[t, part]
        fetch.append(pltpu.make_async_copy(given.at[0, t, part], here, in_sems.at[n]))
        give.append(pltpu.make_async_copy(here, out.at[0, t, part], out_sems.at[n]))
    for copy in fetch:
        copy.start()
    for one, other in zip(fetch, give):
        one.wait()
        other.start()
    for copy in give:
        copy.wait()


def solution(mesh):
    sections, replicas = mesh.shape["section"], mesh.shape["replica"]

    def body(pend, arriving, first, second, gain, bias):
        images, rows, cols, channels = pend.shape[1:]
        pend = jnp.transpose(pend, (0, 2, 3, 1, 4))
        arriving = jnp.transpose(arriving, (0, 2, 3, 1, 4))
        pitch = SLOTS * images
        chunks = channels // LANES
        halves = channels // TILE
        tile = 2 * chunks
        limit = 56 * 2**20
        dma = pltpu.SemaphoreType.DMA
        anywhere = pl.BlockSpec(memory_space=pl.ANY)
        vmem = pl.BlockSpec(memory_space=pltpu.VMEM)
        depth = 9 * channels * channels
        produced = pl.pallas_call(
            functools.partial(kernel, sections, replicas),
            out_shape=jax.ShapeDtypeStruct((1, 2, rows, cols, images, channels), BF16),
            in_specs=[anywhere] * 4 + [vmem] * 2,
            out_specs=anywhere,
            scratch_shapes=[
                pltpu.VMEM((2, chunks, rows, SLOTS, images, LANES), BF16),
                pltpu.VMEM((2, 3, 3, channels, channels), BF16),
                pltpu.VMEM((halves, (rows + 2) * pitch, 3 * TILE), BF16),
                pltpu.VMEM((rows * pitch, channels), F32),
                pltpu.VMEM((chunks, rows, SLOTS, images, LANES), BF16),
                pltpu.VMEM((chunks, rows, SLOTS, images, LANES), BF16),
                pltpu.VMEM((4, tile, LANES), F32),
                pltpu.VMEM((4, replicas - 1, tile, LANES), F32),
                pltpu.VMEM((4, tile, LANES), F32),
                pltpu.VMEM((tile, LANES), F32),
                pltpu.VMEM((2, tile, LANES), F32),
                pltpu.VMEM((2, chunks, rows, SLOTS, images, LANES), BF16),
                dma((2, chunks)),
                dma((2, 3)),
                dma((2, chunks)),
                dma((4,)),
                dma((4,)),
                dma((chunks,)),
                dma((chunks,)),
                dma,
                dma,
            ],
            compiler_params=pltpu.CompilerParams(
                collective_id=0, has_side_effects=True, vmem_limit_bytes=limit
            ),
            cost_estimate=pl.CostEstimate(
                flops=8 * images * rows * cols * depth,
                bytes_accessed=4 * depth,
                transcendentals=0,
            ),
            name="relay",
        )(pend, arriving, first, second, gain, bias)
        produced = pl.pallas_call(
            hand_over,
            out_shape=jax.ShapeDtypeStruct(produced.shape, BF16),
            in_specs=[anywhere],
            out_specs=anywhere,
            scratch_shapes=[pltpu.VMEM(produced.shape[1:], BF16), dma((4,)), dma((4,))],
            compiler_params=pltpu.CompilerParams(vmem_limit_bytes=limit),
            name="hand_over",
        )(produced)
        return jnp.transpose(produced, (0, 1, 4, 2, 3, 5))

    in_specs = (
        P("section", "replica", None, None, None),
        P(None, "replica", None, None, None),
        P("section", None, None, None, None),
        P("section", None, None, None, None),
        P("section", None, None),
        P("section", None, None),
    )
    out_specs = P("section", None, "replica", None, None, None)
    return jax.shard_map(body, mesh=mesh, in_specs=in_specs, out_specs=out_specs, check_vma=False)
```

```python
import functools

import jax
import jax.numpy as jnp
from jax import lax
from jax.experimental import pallas as pl
from jax.experimental.pallas import tpu as pltpu
from jax.sharding import PartitionSpec as P

MESH = pl.DeviceIdType.MESH
F32 = jnp.float32
BF16 = jnp.bfloat16
LANES = 128
SLOTS = 16
TILE = 256


def kernel(
    sections,
    replicas,
    pend,
    arriving,
    first,
    second,
    gain,
    bias,
    out,
    maps,
    weights,
    taps,
    y,
    sent,
    landed,
    mine,
    slots,
    coef,
    moved_coef,
    affine,
    result,
    map_sem,
    weight_sem,
    out_sem,
    stat_send,
    stat_recv,
    bulk_send,
    bulk_recv,
    coef_send,
    coef_recv,
):
    rows, _, images, _ = maps.shape[2:]
    cols, channels = pend.shape[2], pend.shape[4]
    pitch = SLOTS * images
    chunks = channels // LANES
    halves = channels // TILE
    per = TILE // LANES
    cells = images * rows * cols
    sec = lax.axis_index("section")
    me = lax.axis_index("replica")

    barrier = pltpu.get_barrier_semaphore()

    def greet(d, carry):
        peer = lax.rem(me + d, replicas)
        pl.semaphore_signal(
            barrier, inc=1, device_id={"section": sec, "replica": peer}, device_id_type=MESH
        )
        return carry

    lax.fori_loop(1, replicas, greet, 0)

    @pl.when(sec > 0)
    def _():
        pl.semaphore_signal(
            barrier, inc=1, device_id={"section": sec - 1, "replica": me}, device_id_type=MESH
        )

    @pl.when(sec < sections - 1)
    def _():
        pl.semaphore_signal(
            barrier, inc=1, device_id={"section": sec + 1, "replica": me}, device_id_type=MESH
        )

    def lanes(k):
        return slice(k * LANES, (k + 1) * LANES)

    def each(count, step):
        for i in range(count):
            step(i)

    map_copies = [
        [
            pltpu.make_async_copy(
                src.at[0, :, :, :, pl.ds(k * LANES, LANES)],
                maps.at[which, k, :, pl.ds(0, cols)],
                map_sem.at[which, k],
            )
            for k in range(chunks)
        ]
        for which, src in enumerate((pend, arriving))
    ]
    out_copies = [
        [
            pltpu.make_async_copy(
                result.at[tick, k, :, pl.ds(0, cols)],
                out.at[0, tick, :, :, :, pl.ds(k * LANES, LANES)],
                out_sem.at[tick, k],
            )
            for k in range(chunks)
        ]
        for tick in range(2)
    ]
    flat_maps = maps.reshape(2, chunks, rows * pitch, LANES)
    flat_result = result.reshape(2, chunks, rows * pitch, LANES)
    flat_sent = sent.reshape(chunks, rows * pitch, LANES)
    flat_landed = landed.reshape(chunks, rows * pitch, LANES)
    weight_copies = [
        [
            pltpu.make_async_copy(src.at[0, dy], weights.at[layer, dy], weight_sem.at[layer, dy])
            for dy in range(3)
        ]
        for layer, src in enumerate((first, second))
    ]
    for copy in map_copies[0]:
        copy.start()
    for layer in range(2):
        for dy in range(3):
            weight_copies[layer][dy].start()
    for copy in map_copies[1]:
        copy.start()

    for layer in range(2):
        for k in range(chunks):
            lane = slice(k * LANES, (k + 1) * LANES)
            affine[layer, k : k + 1, :] = gain[0, layer : layer + 1, lane]
            affine[layer, chunks + k : chunks + k + 1, :] = bias[0, layer : layer + 1, lane]

    pad = jnp.zeros((halves, pitch, 3 * TILE), BF16)
    taps[:, 0:pitch, :] = pad
    taps[:, (rows + 1) * pitch : (rows + 2) * pitch, :] = pad

    inside = (
        lax.broadcasted_iota(jnp.int32, (rows, pitch, LANES), 1).reshape(rows * pitch, LANES)
        < cols * images
    )

    def lay(k, values):
        flat = jnp.where(inside, values, 0.0)
        half, lane = k // per, (k % per) * LANES
        shifted = (pltpu.roll(flat, images, 0), flat, pltpu.roll(flat, rows * pitch - images, 0))
        for dx, tap in enumerate(shifted):
            at = dx * TILE + lane
            taps[half, pitch : (rows + 1) * pitch, at : at + LANES] = tap.astype(BF16)

    def lay_maps(which):
        each(chunks, lambda k: lay(k, flat_maps[which, k].astype(F32)))

    def multiply(layer, parts, lane=0, width=channels, add=False):
        left = jnp.concatenate(
            [taps[half, dy * pitch : (dy + rows) * pitch, :] for dy, half in parts], axis=1
        )
        right = jnp.concatenate(
            [
                weights[layer, dy, :, half * TILE : (half + 1) * TILE, lane : lane + width].reshape(
                    3 * TILE, width
                )
                for dy, half in parts
            ],
            axis=0,
        )
        total = jnp.dot(left, right, preferred_element_type=F32)
        where = slice(lane, lane + width)
        y[:, where] = y[:, where] + total if add else total

    everything = [(dy, half) for half in range(halves) for dy in range(3)]

    def send_statistics(phase):
        def measure(k):
            total = jnp.sum(jnp.where(inside, y[:, lanes(k)], 0.0), axis=0, keepdims=True)
            mean = total / cells
            centred = jnp.where(inside, y[:, lanes(k)] - mean, 0.0)
            mine[phase, k : k + 1, :] = mean
            mine[phase, chunks + k : chunks + k + 1, :] = jnp.sum(
                centred * centred, axis=0, keepdims=True
            )

        each(chunks, measure)
        if phase == 0:
            pl.semaphore_wait(
                barrier,
                replicas - 1 + has_previous.astype(jnp.int32) + has_next.astype(jnp.int32),
            )

        def send(d, carry):
            peer = lax.rem(me + d, replicas)
            pltpu.make_async_remote_copy(
                src_ref=mine.at[phase],
                dst_ref=slots.at[phase, d - 1],
                send_sem=stat_send.at[phase],
                recv_sem=stat_recv.at[phase],
                device_id={"section": sec, "replica": peer},
                device_id_type=MESH,
            ).start()
            return carry

        lax.fori_loop(1, replicas, send, 0)

    def combine(phase, layer):
        here = slots.at[phase]
        pltpu.make_async_copy(here, here, stat_recv.at[phase]).wait()
        own = mine[phase]
        others = slots[phase]
        total = own + jnp.sum(others, axis=0)
        mean = total[0:chunks] / replicas
        apart = (own[0:chunks] - mean) ** 2 + jnp.sum(
            (others[:, 0:chunks] - mean[None]) ** 2, axis=0
        )
        var = (total[chunks:] + apart * cells) / (cells * replicas)
        scale = affine[layer, 0:chunks, :] * lax.rsqrt(var + 1e-05)
        coef[phase, 0:chunks, :] = scale
        coef[phase, chunks:, :] = affine[layer, chunks:, :] - mean * scale

    def activate(values, table, k):
        scale = table[k : k + 1, :]
        offset = table[chunks + k : chunks + k + 1, :]
        return jnp.maximum(values * scale + offset, 0.0)

    def lay_hidden(phase):
        each(chunks, lambda k: lay(k, activate(y[:, lanes(k)], coef.at[phase], k)))

    def give_result(tick, phase):
        def give(k):
            flat_result[tick, k] = activate(y[:, lanes(k)], coef.at[phase], k).astype(BF16)

        each(chunks, give)
        for copy in out_copies[tick]:
            copy.start()

    def bulk(k):
        return pltpu.make_async_remote_copy(
            src_ref=sent.at[k, :, pl.ds(0, cols)],
            dst_ref=landed.at[k, :, pl.ds(0, cols)],
            send_sem=bulk_send.at[k],
            recv_sem=bulk_recv.at[k],
            device_id={"section": sec + 1, "replica": me},
            device_id_type=MESH,
        )

    def coefficients():
        return pltpu.make_async_remote_copy(
            src_ref=coef.at[1],
            dst_ref=moved_coef,
            send_sem=coef_send,
            recv_sem=coef_recv,
            device_id={"section": sec + 1, "replica": me},
            device_id_type=MESH,
        )

    has_next = sec < sections - 1
    has_previous = sec > 0

    for copy in map_copies[0]:
        copy.wait()
    lay_maps(0)
    for dy in range(3):
        weight_copies[0][dy].wait()
        multiply(0, [(dy, half) for half in range(halves)], add=dy > 0)
    send_statistics(0)
    for dy in range(3):
        weight_copies[1][dy].wait()
    for copy in map_copies[1]:
        copy.wait()
    combine(0, 0)
    lay_hidden(0)

    for g in range(halves):
        multiply(1, everything, g * TILE, TILE)
        for k in range(g * per, (g + 1) * per):
            flat_sent[k] = y[:, k * LANES : (k + 1) * LANES].astype(BF16)

        @pl.when(has_next)
        def _():
            for k in range(g * per, (g + 1) * per):
                if k < chunks - 1:
                    bulk(k).start()

    send_statistics(1)
    combine(1, 1)

    @pl.when(has_next)
    def _():
        coefficients().start()
        bulk(chunks - 1).start()

    give_result(0, 1)

    @pl.when(sec == 0)
    def _():
        lay_maps(1)

    for half in range(halves):

        @pl.when(has_previous)
        def _():
            if half == 0:
                coefficients().wait_recv()
            for k in range(half * per, (half + 1) * per):
                bulk(k).wait_recv()
                lay(k, activate(flat_landed[k].astype(F32), moved_coef, k))

        multiply(0, [(dy, half) for dy in range(3)], add=half > 0)
    send_statistics(2)
    combine(2, 0)
    lay_hidden(2)

    multiply(1, everything)
    send_statistics(3)
    combine(3, 1)
    give_result(1, 3)

    for phase in range(4):
        here = slots.at[phase]
        pltpu.make_async_copy(here, here, stat_send.at[phase]).wait()

    @pl.when(has_next)
    def _():
        for k in range(chunks):
            bulk(k).wait_send()
        coefficients().wait_send()

    for copies in out_copies:
        for copy in copies:
            copy.wait()


def hand_over(given, out, held, in_sems, out_sems):
    ticks, rows = given.shape[1:3]
    cut = (rows + 1) // 2
    parts = [(t, p) for t in range(ticks) for p in (pl.ds(0, cut), pl.ds(cut, rows - cut))]
    fetch, give = [], []
    for n, (t, part) in enumerate(parts):
        here = held.at[t, part]
        fetch.append(pltpu.make_async_copy(given.at[0, t, part], here, in_sems.at[n]))
        give.append(pltpu.make_async_copy(here, out.at[0, t, part], out_sems.at[n]))
    for copy in fetch:
        copy.start()
    for one, other in zip(fetch, give):
        one.wait()
        other.start()
    for copy in give:
        copy.wait()


def solution(mesh):
    sections, replicas = mesh.shape["section"], mesh.shape["replica"]

    def body(pend, arriving, first, second, gain, bias):
        images, rows, cols, channels = pend.shape[1:]
        pend = jnp.transpose(pend, (0, 2, 3, 1, 4))
        arriving = jnp.transpose(arriving, (0, 2, 3, 1, 4))
        pitch = SLOTS * images
        chunks = channels // LANES
        halves = channels // TILE
        tile = 2 * chunks
        limit = 56 * 2**20
        dma = pltpu.SemaphoreType.DMA
        anywhere = pl.BlockSpec(memory_space=pl.ANY)
        vmem = pl.BlockSpec(memory_space=pltpu.VMEM)
        depth = 9 * channels * channels
        produced = pl.pallas_call(
            functools.partial(kernel, sections, replicas),
            out_shape=jax.ShapeDtypeStruct((1, 2, rows, cols, images, channels), BF16),
            in_specs=[anywhere] * 4 + [vmem] * 2,
            out_specs=anywhere,
            scratch_shapes=[
                pltpu.VMEM((2, chunks, rows, SLOTS, images, LANES), BF16),
                pltpu.VMEM((2, 3, 3, channels, channels), BF16),
                pltpu.VMEM((halves, (rows + 2) * pitch, 3 * TILE), BF16),
                pltpu.VMEM((rows * pitch, channels), F32),
                pltpu.VMEM((chunks, rows, SLOTS, images, LANES), BF16),
                pltpu.VMEM((chunks, rows, SLOTS, images, LANES), BF16),
                pltpu.VMEM((4, tile, LANES), F32),
                pltpu.VMEM((4, replicas - 1, tile, LANES), F32),
                pltpu.VMEM((4, tile, LANES), F32),
                pltpu.VMEM((tile, LANES), F32),
                pltpu.VMEM((2, tile, LANES), F32),
                pltpu.VMEM((2, chunks, rows, SLOTS, images, LANES), BF16),
                dma((2, chunks)),
                dma((2, 3)),
                dma((2, chunks)),
                dma((4,)),
                dma((4,)),
                dma((chunks,)),
                dma((chunks,)),
                dma,
                dma,
            ],
            compiler_params=pltpu.CompilerParams(
                collective_id=0, has_side_effects=True, vmem_limit_bytes=limit
            ),
            cost_estimate=pl.CostEstimate(
                flops=8 * images * rows * cols * depth,
                bytes_accessed=4 * depth,
                transcendentals=0,
            ),
            name="relay",
        )(pend, arriving, first, second, gain, bias)
        produced = pl.pallas_call(
            hand_over,
            out_shape=jax.ShapeDtypeStruct(produced.shape, BF16),
            in_specs=[anywhere],
            out_specs=anywhere,
            scratch_shapes=[pltpu.VMEM(produced.shape[1:], BF16), dma((4,)), dma((4,))],
            compiler_params=pltpu.CompilerParams(vmem_limit_bytes=limit),
            name="hand_over",
        )(produced)
        return jnp.transpose(produced, (0, 1, 4, 2, 3, 5))

    in_specs = (
        P("section", "replica", None, None, None),
        P(None, "replica", None, None, None),
        P("section", None, None, None, None),
        P("section", None, None, None, None),
        P("section", None, None),
        P("section", None, None),
    )
    out_specs = P("section", None, "replica", None, None, None)
    return jax.shard_map(body, mesh=mesh, in_specs=in_specs, out_specs=out_specs, check_vma=False)
```

```python
import functools

import jax
import jax.numpy as jnp
from jax import lax
from jax.experimental import pallas as pl
from jax.experimental.pallas import tpu as pltpu
from jax.sharding import PartitionSpec as P

MESH = pl.DeviceIdType.MESH
F32 = jnp.float32
BF16 = jnp.bfloat16
LANES = 128
SLOTS = 16
TILE = 256


def kernel(
    sections,
    replicas,
    pend,
    arriving,
    first,
    second,
    gain,
    bias,
    out,
    maps,
    weights,
    taps,
    y,
    sent,
    landed,
    mine,
    slots,
    coef,
    moved_coef,
    affine,
    result,
    map_sem,
    weight_sem,
    out_sem,
    stat_send,
    stat_recv,
    bulk_send,
    bulk_recv,
    coef_send,
    coef_recv,
):
    rows, _, images, _ = maps.shape[2:]
    cols, channels = pend.shape[2], pend.shape[4]
    pitch = SLOTS * images
    chunks = channels // LANES
    halves = channels // TILE
    per = TILE // LANES
    cells = images * rows * cols
    sec = lax.axis_index("section")
    me = lax.axis_index("replica")

    barrier = pltpu.get_barrier_semaphore()

    def greet(d, carry):
        peer = lax.rem(me + d, replicas)
        pl.semaphore_signal(
            barrier, inc=1, device_id={"section": sec, "replica": peer}, device_id_type=MESH
        )
        return carry

    lax.fori_loop(1, replicas, greet, 0)

    @pl.when(sec > 0)
    def _():
        pl.semaphore_signal(
            barrier, inc=1, device_id={"section": sec - 1, "replica": me}, device_id_type=MESH
        )

    @pl.when(sec < sections - 1)
    def _():
        pl.semaphore_signal(
            barrier, inc=1, device_id={"section": sec + 1, "replica": me}, device_id_type=MESH
        )

    def lanes(k):
        return slice(k * LANES, (k + 1) * LANES)

    def each(count, step):
        for i in range(count):
            step(i)

    map_copies = [
        [
            pltpu.make_async_copy(
                src.at[0, :, :, :, pl.ds(k * LANES, LANES)],
                maps.at[which, k, :, pl.ds(0, cols)],
                map_sem.at[which, k],
            )
            for k in range(chunks)
        ]
        for which, src in enumerate((pend, arriving))
    ]
    out_copies = [
        [
            pltpu.make_async_copy(
                result.at[tick, k, :, pl.ds(0, cols)],
                out.at[0, tick, :, :, :, pl.ds(k * LANES, LANES)],
                out_sem.at[tick, k],
            )
            for k in range(chunks)
        ]
        for tick in range(2)
    ]
    flat_maps = maps.reshape(2, chunks, rows * pitch, LANES)
    flat_result = result.reshape(2, chunks, rows * pitch, LANES)
    flat_sent = sent.reshape(chunks, rows * pitch, LANES)
    flat_landed = landed.reshape(chunks, rows * pitch, LANES)
    weight_copies = [
        [
            pltpu.make_async_copy(src.at[0, dy], weights.at[layer, dy], weight_sem.at[layer, dy])
            for dy in range(3)
        ]
        for layer, src in enumerate((first, second))
    ]
    for copy in map_copies[0]:
        copy.start()
    for layer in range(2):
        for dy in range(3):
            weight_copies[layer][dy].start()
    for copy in map_copies[1]:
        copy.start()

    for layer in range(2):
        for k in range(chunks):
            lane = slice(k * LANES, (k + 1) * LANES)
            affine[layer, k : k + 1, :] = gain[0, layer : layer + 1, lane]
            affine[layer, chunks + k : chunks + k + 1, :] = bias[0, layer : layer + 1, lane]

    pad = jnp.zeros((halves, pitch, 3 * TILE), BF16)
    taps[:, 0:pitch, :] = pad
    taps[:, (rows + 1) * pitch : (rows + 2) * pitch, :] = pad

    inside = (
        lax.broadcasted_iota(jnp.int32, (rows, pitch, LANES), 1).reshape(rows * pitch, LANES)
        < cols * images
    )

    def lay(k, values):
        flat = jnp.where(inside, values, 0.0)
        half, lane = k // per, (k % per) * LANES
        shifted = (pltpu.roll(flat, images, 0), flat, pltpu.roll(flat, rows * pitch - images, 0))
        for dx, tap in enumerate(shifted):
            at = dx * TILE + lane
            taps[half, pitch : (rows + 1) * pitch, at : at + LANES] = tap.astype(BF16)

    def lay_maps(which):
        each(chunks, lambda k: lay(k, flat_maps[which, k].astype(F32)))

    def multiply(layer, parts, lane=0, width=channels, add=False):
        total = None
        for dy, half in parts:
            left = taps[half, dy * pitch : (dy + rows) * pitch, :]
            right = weights[layer, dy, :, half * TILE : (half + 1) * TILE, lane : lane + width]
            term = jnp.dot(left, right.reshape(3 * TILE, width), preferred_element_type=F32)
            total = term if total is None else total + term
        where = slice(lane, lane + width)
        y[:, where] = y[:, where] + total if add else total

    everything = [(dy, half) for half in range(halves) for dy in range(3)]

    def send_statistics(phase):
        def measure(k):
            total = jnp.sum(jnp.where(inside, y[:, lanes(k)], 0.0), axis=0, keepdims=True)
            mean = total / cells
            centred = jnp.where(inside, y[:, lanes(k)] - mean, 0.0)
            mine[phase, k : k + 1, :] = mean
            mine[phase, chunks + k : chunks + k + 1, :] = jnp.sum(
                centred * centred, axis=0, keepdims=True
            )

        each(chunks, measure)
        if phase == 0:
            pl.semaphore_wait(
                barrier,
                replicas - 1 + has_previous.astype(jnp.int32) + has_next.astype(jnp.int32),
            )

        def send(d, carry):
            peer = lax.rem(me + d, replicas)
            pltpu.make_async_remote_copy(
                src_ref=mine.at[phase],
                dst_ref=slots.at[phase, d - 1],
                send_sem=stat_send.at[phase],
                recv_sem=stat_recv.at[phase],
                device_id={"section": sec, "replica": peer},
                device_id_type=MESH,
            ).start()
            return carry

        lax.fori_loop(1, replicas, send, 0)

    def combine(phase, layer):
        here = slots.at[phase]
        pltpu.make_async_copy(here, here, stat_recv.at[phase]).wait()
        own = mine[phase]
        others = slots[phase]
        total = own + jnp.sum(others, axis=0)
        mean = total[0:chunks] / replicas
        apart = (own[0:chunks] - mean) ** 2 + jnp.sum(
            (others[:, 0:chunks] - mean[None]) ** 2, axis=0
        )
        var = (total[chunks:] + apart * cells) / (cells * replicas)
        scale = affine[layer, 0:chunks, :] * lax.rsqrt(var + 1e-05)
        coef[phase, 0:chunks, :] = scale
        coef[phase, chunks:, :] = affine[layer, chunks:, :] - mean * scale

    def activate(values, table, k):
        scale = table[k : k + 1, :]
        offset = table[chunks + k : chunks + k + 1, :]
        return jnp.maximum(values * scale + offset, 0.0)

    def lay_hidden(phase):
        each(chunks, lambda k: lay(k, activate(y[:, lanes(k)], coef.at[phase], k)))

    def give_result(tick, phase):
        def give(k):
            flat_result[tick, k] = activate(y[:, lanes(k)], coef.at[phase], k).astype(BF16)

        each(chunks, give)
        for copy in out_copies[tick]:
            copy.start()

    def bulk(k):
        return pltpu.make_async_remote_copy(
            src_ref=sent.at[k, :, pl.ds(0, cols)],
            dst_ref=landed.at[k, :, pl.ds(0, cols)],
            send_sem=bulk_send.at[k],
            recv_sem=bulk_recv.at[k],
            device_id={"section": sec + 1, "replica": me},
            device_id_type=MESH,
        )

    def coefficients():
        return pltpu.make_async_remote_copy(
            src_ref=coef.at[1],
            dst_ref=moved_coef,
            send_sem=coef_send,
            recv_sem=coef_recv,
            device_id={"section": sec + 1, "replica": me},
            device_id_type=MESH,
        )

    has_next = sec < sections - 1
    has_previous = sec > 0

    for copy in map_copies[0]:
        copy.wait()
    lay_maps(0)
    for dy in range(3):
        weight_copies[0][dy].wait()
        multiply(0, [(dy, half) for half in range(halves)], add=dy > 0)
    send_statistics(0)
    for dy in range(3):
        weight_copies[1][dy].wait()
    for copy in map_copies[1]:
        copy.wait()
    combine(0, 0)
    lay_hidden(0)

    for g in range(halves):
        multiply(1, everything, g * TILE, TILE)
        for k in range(g * per, (g + 1) * per):
            flat_sent[k] = y[:, k * LANES : (k + 1) * LANES].astype(BF16)

        @pl.when(has_next)
        def _():
            for k in range(g * per, (g + 1) * per):
                if k < chunks - 1:
                    bulk(k).start()

    send_statistics(1)
    combine(1, 1)

    @pl.when(has_next)
    def _():
        coefficients().start()
        bulk(chunks - 1).start()

    give_result(0, 1)

    @pl.when(sec == 0)
    def _():
        lay_maps(1)

    for half in range(halves):

        @pl.when(has_previous)
        def _():
            if half == 0:
                coefficients().wait_recv()
            for k in range(half * per, (half + 1) * per):
                bulk(k).wait_recv()
                lay(k, activate(flat_landed[k].astype(F32), moved_coef, k))

        multiply(0, [(dy, half) for dy in range(3)], add=half > 0)
    send_statistics(2)
    combine(2, 0)
    lay_hidden(2)

    multiply(1, everything)
    send_statistics(3)
    combine(3, 1)
    give_result(1, 3)

    for phase in range(4):
        here = slots.at[phase]
        pltpu.make_async_copy(here, here, stat_send.at[phase]).wait()

    @pl.when(has_next)
    def _():
        for k in range(chunks):
            bulk(k).wait_send()
        coefficients().wait_send()

    for copies in out_copies:
        for copy in copies:
            copy.wait()


def hand_over(given, out, held, in_sems, out_sems):
    ticks, rows = given.shape[1:3]
    cut = (rows + 1) // 2
    parts = [(t, p) for t in range(ticks) for p in (pl.ds(0, cut), pl.ds(cut, rows - cut))]
    fetch, give = [], []
    for n, (t, part) in enumerate(parts):
        here = held.at[t, part]
        fetch.append(pltpu.make_async_copy(given.at[0, t, part], here, in_sems.at[n]))
        give.append(pltpu.make_async_copy(here, out.at[0, t, part], out_sems.at[n]))
    for copy in fetch:
        copy.start()
    for one, other in zip(fetch, give):
        one.wait()
        other.start()
    for copy in give:
        copy.wait()


def solution(mesh):
    sections, replicas = mesh.shape["section"], mesh.shape["replica"]

    def body(pend, arriving, first, second, gain, bias):
        images, rows, cols, channels = pend.shape[1:]
        pend = jnp.transpose(pend, (0, 2, 3, 1, 4))
        arriving = jnp.transpose(arriving, (0, 2, 3, 1, 4))
        pitch = SLOTS * images
        chunks = channels // LANES
        halves = channels // TILE
        tile = 2 * chunks
        limit = 56 * 2**20
        dma = pltpu.SemaphoreType.DMA
        anywhere = pl.BlockSpec(memory_space=pl.ANY)
        vmem = pl.BlockSpec(memory_space=pltpu.VMEM)
        depth = 9 * channels * channels
        produced = pl.pallas_call(
            functools.partial(kernel, sections, replicas),
            out_shape=jax.ShapeDtypeStruct((1, 2, rows, cols, images, channels), BF16),
            in_specs=[anywhere] * 4 + [vmem] * 2,
            out_specs=anywhere,
            scratch_shapes=[
                pltpu.VMEM((2, chunks, rows, SLOTS, images, LANES), BF16),
                pltpu.VMEM((2, 3, 3, channels, channels), BF16),
                pltpu.VMEM((halves, (rows + 2) * pitch, 3 * TILE), BF16),
                pltpu.VMEM((rows * pitch, channels), F32),
                pltpu.VMEM((chunks, rows, SLOTS, images, LANES), BF16),
                pltpu.VMEM((chunks, rows, SLOTS, images, LANES), BF16),
                pltpu.VMEM((4, tile, LANES), F32),
                pltpu.VMEM((4, replicas - 1, tile, LANES), F32),
                pltpu.VMEM((4, tile, LANES), F32),
                pltpu.VMEM((tile, LANES), F32),
                pltpu.VMEM((2, tile, LANES), F32),
                pltpu.VMEM((2, chunks, rows, SLOTS, images, LANES), BF16),
                dma((2, chunks)),
                dma((2, 3)),
                dma((2, chunks)),
                dma((4,)),
                dma((4,)),
                dma((chunks,)),
                dma((chunks,)),
                dma,
                dma,
            ],
            compiler_params=pltpu.CompilerParams(
                collective_id=0, has_side_effects=True, vmem_limit_bytes=limit
            ),
            cost_estimate=pl.CostEstimate(
                flops=8 * images * rows * cols * depth,
                bytes_accessed=4 * depth,
                transcendentals=0,
            ),
            name="relay",
        )(pend, arriving, first, second, gain, bias)
        produced = pl.pallas_call(
            hand_over,
            out_shape=jax.ShapeDtypeStruct(produced.shape, BF16),
            in_specs=[anywhere],
            out_specs=anywhere,
            scratch_shapes=[pltpu.VMEM(produced.shape[1:], BF16), dma((4,)), dma((4,))],
            compiler_params=pltpu.CompilerParams(vmem_limit_bytes=limit),
            name="hand_over",
        )(produced)
        return jnp.transpose(produced, (0, 1, 4, 2, 3, 5))

    in_specs = (
        P("section", "replica", None, None, None),
        P(None, "replica", None, None, None),
        P("section", None, None, None, None),
        P("section", None, None, None, None),
        P("section", None, None),
        P("section", None, None),
    )
    out_specs = P("section", None, "replica", None, None, None)
    return jax.shard_map(body, mesh=mesh, in_specs=in_specs, out_specs=out_specs, check_vma=False)
```

```python
import functools

import jax
import jax.numpy as jnp
from jax import lax
from jax.experimental import pallas as pl
from jax.experimental.pallas import tpu as pltpu
from jax.sharding import PartitionSpec as P

MESH = pl.DeviceIdType.MESH
F32 = jnp.float32
BF16 = jnp.bfloat16
LANES = 128
SLOTS = 16
TILE = 256


def kernel(
    sections,
    replicas,
    pend,
    arriving,
    first,
    second,
    gain,
    bias,
    out,
    maps,
    weights,
    taps,
    y,
    sent,
    landed,
    mine,
    slots,
    coef,
    moved_coef,
    affine,
    result,
    map_sem,
    weight_sem,
    out_sem,
    stat_send,
    stat_recv,
    bulk_send,
    bulk_recv,
    coef_send,
    coef_recv,
):
    rows, _, images, _ = maps.shape[2:]
    cols, channels = pend.shape[2], pend.shape[4]
    pitch = SLOTS * images
    chunks = channels // LANES
    halves = channels // TILE
    per = TILE // LANES
    cells = images * rows * cols
    sec = lax.axis_index("section")
    me = lax.axis_index("replica")

    barrier = pltpu.get_barrier_semaphore()

    def greet(d, carry):
        peer = lax.rem(me + d, replicas)
        pl.semaphore_signal(
            barrier, inc=1, device_id={"section": sec, "replica": peer}, device_id_type=MESH
        )
        return carry

    lax.fori_loop(1, replicas, greet, 0)

    @pl.when(sec > 0)
    def _():
        pl.semaphore_signal(
            barrier, inc=1, device_id={"section": sec - 1, "replica": me}, device_id_type=MESH
        )

    @pl.when(sec < sections - 1)
    def _():
        pl.semaphore_signal(
            barrier, inc=1, device_id={"section": sec + 1, "replica": me}, device_id_type=MESH
        )

    def lanes(k):
        return slice(k * LANES, (k + 1) * LANES)

    def each(count, step):
        for i in range(count):
            step(i)

    map_copies = [
        [
            pltpu.make_async_copy(
                src.at[0, :, :, :, pl.ds(k * LANES, LANES)],
                maps.at[which, k, :, pl.ds(0, cols)],
                map_sem.at[which, k],
            )
            for k in range(chunks)
        ]
        for which, src in enumerate((pend, arriving))
    ]
    out_copies = [
        [
            pltpu.make_async_copy(
                result.at[tick, k, :, pl.ds(0, cols)],
                out.at[0, tick, :, :, :, pl.ds(k * LANES, LANES)],
                out_sem.at[tick, k],
            )
            for k in range(chunks)
        ]
        for tick in range(2)
    ]
    flat_maps = maps.reshape(2, chunks, rows * pitch, LANES)
    flat_result = result.reshape(2, chunks, rows * pitch, LANES)
    flat_sent = sent.reshape(chunks, rows * pitch, LANES)
    flat_landed = landed.reshape(chunks, rows * pitch, LANES)
    weight_copies = [
        [
            pltpu.make_async_copy(src.at[0, dy], weights.at[layer, dy], weight_sem.at[layer, dy])
            for dy in range(3)
        ]
        for layer, src in enumerate((first, second))
    ]
    for copy in map_copies[0]:
        copy.start()
    for layer in range(2):
        for dy in range(3):
            weight_copies[layer][dy].start()
    for copy in map_copies[1]:
        copy.start()

    for layer in range(2):
        for k in range(chunks):
            lane = slice(k * LANES, (k + 1) * LANES)
            affine[layer, k : k + 1, :] = gain[0, layer : layer + 1, lane]
            affine[layer, chunks + k : chunks + k + 1, :] = bias[0, layer : layer + 1, lane]

    pad = jnp.zeros((halves, pitch, 3 * TILE), BF16)
    taps[:, 0:pitch, :] = pad
    taps[:, (rows + 1) * pitch : (rows + 2) * pitch, :] = pad

    inside = (
        lax.broadcasted_iota(jnp.int32, (rows, pitch, LANES), 1).reshape(rows * pitch, LANES)
        < cols * images
    )

    def lay(k, values):
        flat = jnp.where(inside, values, 0.0)
        half, lane = k // per, (k % per) * LANES
        shifted = (pltpu.roll(flat, images, 0), flat, pltpu.roll(flat, rows * pitch - images, 0))
        for dx, tap in enumerate(shifted):
            at = dx * TILE + lane
            taps[half, pitch : (rows + 1) * pitch, at : at + LANES] = tap.astype(BF16)

    def lay_maps(which):
        each(chunks, lambda k: lay(k, flat_maps[which, k].astype(F32)))

    def multiply(layer, parts, lane=0, width=channels, add=False):
        total = None
        for dy, half in parts:
            left = taps[half, dy * pitch : (dy + rows) * pitch, :]
            right = weights[layer, dy, :, half * TILE : (half + 1) * TILE, lane : lane + width]
            term = jnp.dot(left, right.reshape(3 * TILE, width), preferred_element_type=F32)
            total = term if total is None else total + term
        where = slice(lane, lane + width)
        y[:, where] = y[:, where] + total if add else total

    everything = [(dy, half) for half in range(halves) for dy in range(3)]

    def send_statistics(phase):
        def measure(k):
            total = jnp.sum(jnp.where(inside, y[:, lanes(k)], 0.0), axis=0, keepdims=True)
            mean = total / cells
            centred = jnp.where(inside, y[:, lanes(k)] - mean, 0.0)
            mine[phase, k : k + 1, :] = mean
            mine[phase, chunks + k : chunks + k + 1, :] = jnp.sum(
                centred * centred, axis=0, keepdims=True
            )

        each(chunks, measure)
        if phase == 0:
            pl.semaphore_wait(
                barrier,
                replicas - 1 + has_previous.astype(jnp.int32) + has_next.astype(jnp.int32),
            )

        def send(d, carry):
            peer = lax.rem(me + d, replicas)
            pltpu.make_async_remote_copy(
                src_ref=mine.at[phase],
                dst_ref=slots.at[phase, d - 1],
                send_sem=stat_send.at[phase],
                recv_sem=stat_recv.at[phase],
                device_id={"section": sec, "replica": peer},
                device_id_type=MESH,
            ).start()
            return carry

        lax.fori_loop(1, replicas, send, 0)

    def combine(phase, layer):
        here = slots.at[phase]
        pltpu.make_async_copy(here, here, stat_recv.at[phase]).wait()
        own = mine[phase]
        others = slots[phase]
        total = own + jnp.sum(others, axis=0)
        mean = total[0:chunks] / replicas
        apart = (own[0:chunks] - mean) ** 2 + jnp.sum(
            (others[:, 0:chunks] - mean[None]) ** 2, axis=0
        )
        var = (total[chunks:] + apart * cells) / (cells * replicas)
        scale = affine[layer, 0:chunks, :] * lax.rsqrt(var + 1e-05)
        coef[phase, 0:chunks, :] = scale
        coef[phase, chunks:, :] = affine[layer, chunks:, :] - mean * scale

    def activate(values, table, k):
        scale = table[k : k + 1, :]
        offset = table[chunks + k : chunks + k + 1, :]
        return jnp.maximum(values * scale + offset, 0.0)

    def lay_hidden(phase):
        each(chunks, lambda k: lay(k, activate(y[:, lanes(k)], coef.at[phase], k)))

    def give_result(tick, phase):
        def give(k):
            flat_result[tick, k] = activate(y[:, lanes(k)], coef.at[phase], k).astype(BF16)

        each(chunks, give)
        for copy in out_copies[tick]:
            copy.start()

    def bulk(k):
        return pltpu.make_async_remote_copy(
            src_ref=sent.at[k, :, pl.ds(0, cols)],
            dst_ref=landed.at[k, :, pl.ds(0, cols)],
            send_sem=bulk_send.at[k],
            recv_sem=bulk_recv.at[k],
            device_id={"section": sec + 1, "replica": me},
            device_id_type=MESH,
        )

    def coefficients():
        return pltpu.make_async_remote_copy(
            src_ref=coef.at[1],
            dst_ref=moved_coef,
            send_sem=coef_send,
            recv_sem=coef_recv,
            device_id={"section": sec + 1, "replica": me},
            device_id_type=MESH,
        )

    has_next = sec < sections - 1
    has_previous = sec > 0

    for copy in map_copies[0]:
        copy.wait()
    lay_maps(0)
    for dy in range(3):
        weight_copies[0][dy].wait()
        multiply(0, [(dy, half) for half in range(halves)], add=dy > 0)
    send_statistics(0)
    for dy in range(3):
        weight_copies[1][dy].wait()
    for copy in map_copies[1]:
        copy.wait()
    combine(0, 0)
    lay_hidden(0)

    multiply(1, everything)
    for k in range(chunks):
        flat_sent[k] = y[:, k * LANES : (k + 1) * LANES].astype(BF16)

        @pl.when(has_next)
        def _():
            if k < chunks - 1:
                bulk(k).start()

    send_statistics(1)
    combine(1, 1)

    @pl.when(has_next)
    def _():
        coefficients().start()
        bulk(chunks - 1).start()

    give_result(0, 1)

    @pl.when(sec == 0)
    def _():
        lay_maps(1)

    for half in range(halves):

        @pl.when(has_previous)
        def _():
            if half == 0:
                coefficients().wait_recv()
            for k in range(half * per, (half + 1) * per):
                bulk(k).wait_recv()
                lay(k, activate(flat_landed[k].astype(F32), moved_coef, k))

        multiply(0, [(dy, half) for dy in range(3)], add=half > 0)
    send_statistics(2)
    combine(2, 0)
    lay_hidden(2)

    multiply(1, everything)
    send_statistics(3)
    combine(3, 1)
    give_result(1, 3)

    for phase in range(4):
        here = slots.at[phase]
        pltpu.make_async_copy(here, here, stat_send.at[phase]).wait()

    @pl.when(has_next)
    def _():
        for k in range(chunks):
            bulk(k).wait_send()
        coefficients().wait_send()

    for copies in out_copies:
        for copy in copies:
            copy.wait()


def hand_over(given, out, held, in_sems, out_sems):
    ticks, rows = given.shape[1:3]
    cut = (rows + 1) // 2
    parts = [(t, p) for t in range(ticks) for p in (pl.ds(0, cut), pl.ds(cut, rows - cut))]
    fetch, give = [], []
    for n, (t, part) in enumerate(parts):
        here = held.at[t, part]
        fetch.append(pltpu.make_async_copy(given.at[0, t, part], here, in_sems.at[n]))
        give.append(pltpu.make_async_copy(here, out.at[0, t, part], out_sems.at[n]))
    for copy in fetch:
        copy.start()
    for one, other in zip(fetch, give):
        one.wait()
        other.start()
    for copy in give:
        copy.wait()


def solution(mesh):
    sections, replicas = mesh.shape["section"], mesh.shape["replica"]

    def body(pend, arriving, first, second, gain, bias):
        images, rows, cols, channels = pend.shape[1:]
        pend = jnp.transpose(pend, (0, 2, 3, 1, 4))
        arriving = jnp.transpose(arriving, (0, 2, 3, 1, 4))
        pitch = SLOTS * images
        chunks = channels // LANES
        halves = channels // TILE
        tile = 2 * chunks
        limit = 56 * 2**20
        dma = pltpu.SemaphoreType.DMA
        anywhere = pl.BlockSpec(memory_space=pl.ANY)
        vmem = pl.BlockSpec(memory_space=pltpu.VMEM)
        depth = 9 * channels * channels
        produced = pl.pallas_call(
            functools.partial(kernel, sections, replicas),
            out_shape=jax.ShapeDtypeStruct((1, 2, rows, cols, images, channels), BF16),
            in_specs=[anywhere] * 4 + [vmem] * 2,
            out_specs=anywhere,
            scratch_shapes=[
                pltpu.VMEM((2, chunks, rows, SLOTS, images, LANES), BF16),
                pltpu.VMEM((2, 3, 3, channels, channels), BF16),
                pltpu.VMEM((halves, (rows + 2) * pitch, 3 * TILE), BF16),
                pltpu.VMEM((rows * pitch, channels), F32),
                pltpu.VMEM((chunks, rows, SLOTS, images, LANES), BF16),
                pltpu.VMEM((chunks, rows, SLOTS, images, LANES), BF16),
                pltpu.VMEM((4, tile, LANES), F32),
                pltpu.VMEM((4, replicas - 1, tile, LANES), F32),
                pltpu.VMEM((4, tile, LANES), F32),
                pltpu.VMEM((tile, LANES), F32),
                pltpu.VMEM((2, tile, LANES), F32),
                pltpu.VMEM((2, chunks, rows, SLOTS, images, LANES), BF16),
                dma((2, chunks)),
                dma((2, 3)),
                dma((2, chunks)),
                dma((4,)),
                dma((4,)),
                dma((chunks,)),
                dma((chunks,)),
                dma,
                dma,
            ],
            compiler_params=pltpu.CompilerParams(
                collective_id=0, has_side_effects=True, vmem_limit_bytes=limit
            ),
            cost_estimate=pl.CostEstimate(
                flops=8 * images * rows * cols * depth,
                bytes_accessed=4 * depth,
                transcendentals=0,
            ),
            name="relay",
        )(pend, arriving, first, second, gain, bias)
        produced = pl.pallas_call(
            hand_over,
            out_shape=jax.ShapeDtypeStruct(produced.shape, BF16),
            in_specs=[anywhere],
            out_specs=anywhere,
            scratch_shapes=[pltpu.VMEM(produced.shape[1:], BF16), dma((4,)), dma((4,))],
            compiler_params=pltpu.CompilerParams(vmem_limit_bytes=limit),
            name="hand_over",
        )(produced)
        return jnp.transpose(produced, (0, 1, 4, 2, 3, 5))

    in_specs = (
        P("section", "replica", None, None, None),
        P(None, "replica", None, None, None),
        P("section", None, None, None, None),
        P("section", None, None, None, None),
        P("section", None, None),
        P("section", None, None),
    )
    out_specs = P("section", None, "replica", None, None, None)
    return jax.shard_map(body, mesh=mesh, in_specs=in_specs, out_specs=out_specs, check_vma=False)
```
